128 devices in a mesh: tp: 16 (over y, z_lo, core), dp: 8 (over x, z_hi).
Axes of the slice: x: 4, y: 4, z: 4 (z_hi: 2, z_lo: 2; z = z_hi * 2 + z_lo), core: 2. Of those that a mesh axis runs over, the one named last changes fastest.
Arguments:
- tokens: bfloat16 [16, 1024, 2048], P('dp', 'tp'), may hold values from -6 to 6
- lengths: int32 [16], P('dp'), may hold values from 150 to 1024, as said below
- exit_layers: int32 [16, 1024], P('dp'), may hold values from 1 to 24
- weight_query: bfloat16 [2048, 2048], P(None, 'tp'), may hold values from -0.125 to 0.125
- bias_query: float32 [2048], P('tp'), may hold values from -3 to 3
- weight_key: bfloat16 [2048, 2048], P(None, 'tp'), may hold values from -0.125 to 0.125
- weight_value: bfloat16 [2048, 2048], P(None, 'tp'), may hold values from -0.125 to 0.125
- bias_value: float32 [2048], P('tp'), may hold values from -3 to 3
- weight_out: bfloat16 [2048, 2048], P('tp'), may hold values from -2 to 2
- bias_out: float32 [2048], replicated, may hold values from -3 to 3
- weight_up: bfloat16 [2048, 8192], P(None, 'tp'), may hold values from -0.125 to 0.125
- bias_up: float32 [8192], P('tp'), may hold values from -3 to 3
- weight_down: bfloat16 [8192, 2048], P('tp'), may hold values from -0.0625 to 0.0625
- bias_down: float32 [2048], replicated, may hold values from -3 to 3
- gain_in: float32 [2048], replicated, may hold values from 0.25 to 1.75
- shift_in: float32 [2048], replicated, may hold values from -2 to 2
- gain_mid: float32 [2048], replicated, may hold values from 0.25 to 1.75
- shift_mid: float32 [2048], replicated, may hold values from -2 to 2
- cotangent: bfloat16 [16, 1024, 2048], P('dp', 'tp'), may hold values from -6 to 6
Outputs:
- output: bfloat16 [16, 1024, 2048], P('dp', 'tp')
- grad_tokens: float32 [16, 1024, 2048], P('dp', 'tp')
- grad_weight_query: float32 [2048, 2048], P('dp', 'tp')
- grad_bias_query: float32 [2048], P(('tp', 'dp'))
- grad_weight_key: float32 [2048, 2048], P('dp', 'tp')
- grad_weight_value: float32 [2048, 2048], P('dp', 'tp')
- grad_bias_value: float32 [2048], P(('tp', 'dp'))
- grad_weight_out: float32 [2048, 2048], P('tp', 'dp')
- grad_bias_out: float32 [2048], P('dp')
- grad_weight_up: float32 [2048, 8192], P('dp', 'tp')
- grad_bias_up: float32 [8192], P(('tp', 'dp'))
- grad_weight_down: float32 [8192, 2048], P('tp', 'dp')
- grad_bias_down: float32 [2048], P('dp')
- grad_gain_in: float32 [2048], P('dp')
- grad_shift_in: float32 [2048], P('dp')
- grad_gain_mid: float32 [2048], P('dp')
- grad_shift_mid: float32 [2048], P('dp')
The draws below stay inside these ranges and needn't reach their ends.
Inputs may be any that keep to these rules, and one draw needn't show every extreme that they name: `lengths`: among the 2 sequences of one index of dp, one drawn from the seed has length 1024.
All inputs are finite; a program needn't handle non-finite values.
Results may differ from the reference program's by a relative error of at most 0.035.
Values may be sent and summed in bfloat16 or wider, within the bound.
No kernel may reach another device: no remote copies, remote signals or barrier semaphores. Data moves between devices by JAX's collectives and lax.ppermute only.
A program may use at most 192 MiB of HBM per device.

```python
import jax
import jax.numpy as jnp
from jax import lax

D = 2048
HEADS = 32
HEAD = 64
FF = 8192
NLAYERS = 24
LAYER = 12
SEQ_LEN = 1024
MIN_LEN = 150
SEQS = 2
BATCH = 16
N_TP = 16


def draw_lengths(key, part):
    groups = BATCH // SEQS
    first_key, second_key, third_key = jax.random.split(jax.random.fold_in(key, 17), 3)
    extent = SEQ_LEN - MIN_LEN
    first_draw = jax.random.randint(first_key, (groups, SEQS), 0, extent + 1)
    second_draw = jax.random.randint(second_key, (groups, SEQS), 0, extent + 1)
    drawn = MIN_LEN + first_draw * second_draw // max(extent, 1)
    chosen = jax.random.randint(third_key, (groups, 1), 0, SEQS)
    drawn = jnp.where(jnp.arange(SEQS)[None, :] == chosen, SEQ_LEN, drawn)
    return drawn.reshape(-1).astype(jnp.int32)


def touch_ends(values, rng, least, largest):
    shape = values.shape
    spot = [jax.random.randint(jax.random.fold_in(rng, axis), (), 0, shape[axis]) for axis in range(len(shape))]
    values = values.at[tuple(spot)].set(least)
    longest = shape.index(max(shape))
    spot[longest] = (spot[longest] + 1) % shape[longest]
    return values.at[tuple(spot)].set(largest)


def level_of(own_key, shape, pieces, smallest, high):
    def one(axis_at, blocks):
        steps = jax.random.uniform(jax.random.fold_in(jax.random.fold_in(own_key, 6), axis_at), (blocks,), jnp.float32, smallest / len(pieces), high / len(pieces))
        return jnp.repeat(jnp.exp(steps), shape[axis_at] // blocks).reshape((-1,) + (1,) * (len(shape) - axis_at - 1))

    gain = one(*pieces[0])
    for cut in pieces[1:]:
        gain = gain * one(*cut)
    return gain


def gaussian(stream_key, dims, spread, bound, cuts=(), dtype=jnp.bfloat16):
    values = spread * jax.random.normal(stream_key, dims, jnp.float32)
    if cuts:
        values = values * level_of(stream_key, dims, cuts, -0.22, 0.18)
    return jnp.clip(values, -bound, bound).astype(dtype)


def setup_inputs(seed: int = 0) -> dict:
    arg_keys = jax.random.split(jax.random.key(seed), 20)
    return {
        "tokens": gaussian(arg_keys[0], (BATCH, SEQ_LEN, D), 1.0, 6.0, ((0, 8), (1, 16))),
        "lengths": draw_lengths(jax.random.fold_in(arg_keys[19], 71), 0),
        "exit_layers": touch_ends(jax.random.randint(arg_keys[2], (BATCH, SEQ_LEN), 1, NLAYERS + 1), jax.random.fold_in(arg_keys[2], 1), 1, NLAYERS).astype(jnp.int32),
        "weight_query": gaussian(arg_keys[3], (D, D), D ** -0.5, 0.125, ((1, 16),)),
        "bias_query": gaussian(arg_keys[4], (D,), 0.5, 3.0, ((0, 16),), jnp.float32),
        "weight_key": gaussian(arg_keys[5], (D, D), D ** -0.5, 0.125, ((1, 16),)),
        "weight_value": gaussian(arg_keys[6], (D, D), D ** -0.5, 0.125, ((1, 16),)),
        "bias_value": gaussian(arg_keys[7], (D,), 0.5, 3.0, ((0, 16),), jnp.float32),
        "weight_out": gaussian(arg_keys[8], (D, D), (max(1, 4 * D // SEQ_LEN)) ** -0.5, 2.0, ((0, 16),)),
        "bias_out": gaussian(arg_keys[9], (D,), 0.5, 3.0, (), jnp.float32),
        "weight_up": gaussian(arg_keys[10], (D, FF), D ** -0.5, 0.125, ((1, 16),)),
        "bias_up": gaussian(arg_keys[11], (FF,), 0.5, 3.0, ((0, 16),), jnp.float32),
        "weight_down": gaussian(arg_keys[12], (FF, D), FF ** -0.5, 0.0625, ((0, 16),)),
        "bias_down": gaussian(arg_keys[13], (D,), 0.5, 3.0, (), jnp.float32),
        "gain_in": jnp.clip(1.0 + 0.15 * jax.random.normal(arg_keys[14], (D,), jnp.float32), 0.25, 1.75),
        "shift_in": gaussian(arg_keys[15], (D,), 0.3, 2.0, (), jnp.float32),
        "gain_mid": jnp.clip(1.0 + 0.15 * jax.random.normal(arg_keys[16], (D,), jnp.float32), 0.25, 1.75),
        "shift_mid": gaussian(arg_keys[17], (D,), 0.3, 2.0, (), jnp.float32),
        "cotangent": gaussian(arg_keys[18], (BATCH, SEQ_LEN, D), 1.0, 6.0, ((0, 8), (1, 16))),
    }


EPS = 1e-05
MASKED = -1e+30
PRECISE = lax.Precision.HIGHEST
block_rows = 512

@jax.custom_vjp
def low(v):
    return lax.optimization_barrier(v.astype(jnp.bfloat16)).astype(jnp.float32)

@jax.custom_vjp
def low_back(v):
    return v

def low_keep(v):
    return (low(v), None)

def low_pass(kept, grad):
    return (grad,)

def back_keep(v):
    return (v, None)

def back_low(kept, grad):
    return (low(grad),)
low.defvjp(low_keep, low_pass)
low_back.defvjp(back_keep, back_low)

def norm_rows(values, norm_gain, norm_bias):
    average = lax.optimization_barrier(jnp.mean(values, -1, keepdims=True))
    centred = values - average
    variance = lax.optimization_barrier(jnp.mean(centred * centred, -1, keepdims=True))
    return centred * lax.rsqrt(variance + EPS) * norm_gain + norm_bias

def attend_block(query_block, offset, key_vecs, value_vecs, length):
    row_index = offset + jnp.arange(query_block.shape[0]).astype(jnp.int32)
    column_index = jnp.arange(key_vecs.shape[0]).astype(jnp.int32)
    allowed = (column_index[None, :] <= row_index[:, None]) & (column_index[None, :] < length)
    scores = low_back(jnp.einsum('qhd,khd->hqk', query_block, key_vecs, precision=PRECISE))
    scores = jnp.where(allowed[None], scores, MASKED)
    row_max = lax.optimization_barrier(jnp.max(scores, -1, keepdims=True))
    exponent = jnp.exp(scores - row_max)
    soft_weights = low(exponent / lax.optimization_barrier(jnp.sum(exponent, -1, keepdims=True)))
    return jnp.einsum('hqk,khd->qhd', soft_weights, value_vecs, precision=PRECISE)

def decoder_layer(hidden, live, length, params):
    w_query, b_query, w_key, w_value, b_value, w_out, b_out, w_up, b_up, w_down, b_down, g_in, s_in, g_mid, s_mid = params
    seq_len = hidden.shape[0]
    hidden_in = low(norm_rows(hidden, g_in, s_in))
    queries = low(low_back((jnp.dot(hidden_in, w_query, precision=PRECISE) + b_query) * HEAD ** (-0.5)))
    key_vecs = low(low_back(jnp.dot(hidden_in, w_key, precision=PRECISE)))
    value_vecs = low(low_back(jnp.dot(hidden_in, w_value, precision=PRECISE) + b_value))
    block_len = min(block_rows, seq_len)
    blocks = seq_len // block_len
    query_blocks = queries.reshape(blocks, block_len, HEADS, HEAD)
    key_vecs = key_vecs.reshape(seq_len, HEADS, HEAD)
    value_vecs = value_vecs.reshape(seq_len, HEADS, HEAD)
    offsets = (jnp.arange(blocks) * block_len).astype(jnp.int32)
    checked = jax.checkpoint(attend_block)
    context = lax.map(lambda packed: checked(packed[0], packed[1], key_vecs, value_vecs, length), (query_blocks, offsets))
    context = low(low_back(context.reshape(seq_len, HEADS * HEAD)))
    parts = jnp.einsum('lgc,gcd->gld', context.reshape(seq_len, N_TP, -1), w_out.reshape(N_TP, -1, w_out.shape[1]), precision=PRECISE)
    attention = low_back(lax.optimization_barrier(jnp.sum(low(parts), 0)))
    mid = hidden + live[:, None] * (attention + b_out)
    hidden_mid = low(norm_rows(mid, g_mid, s_mid))
    up_sum = low_back(jnp.dot(hidden_mid, w_up, precision=PRECISE) + b_up)
    activated = low(jax.nn.gelu(up_sum))
    down_parts = jnp.einsum('lgf,gfd->gld', activated.reshape(seq_len, N_TP, -1), w_down.reshape(N_TP, -1, w_down.shape[1]), precision=PRECISE)
    branch = low_back(lax.optimization_barrier(jnp.sum(low(down_parts), 0)))
    return mid + live[:, None] * (branch + b_down)

def reference(tokens, lengths, exit_layers, weight_query, bias_query, weight_key, weight_value, bias_value, weight_out, bias_out, weight_up, bias_up, weight_down, bias_down, gain_in, shift_in, gain_mid, shift_mid, cotangent):
    params = tuple((param.astype(jnp.float32) for param in (weight_query, bias_query, weight_key, weight_value, bias_value, weight_out, bias_out, weight_up, bias_up, weight_down, bias_down, gain_in, shift_in, gain_mid, shift_mid)))
    positions = jnp.arange(SEQ_LEN).astype(jnp.int32)

    def one_sequence(totals, packed):
        hidden, upstream, length, exit_row = packed
        live = ((positions < length) & (exit_row >= LAYER)).astype(jnp.float32)
        result, pull = jax.vjp(lambda inner_x, inner_p: decoder_layer(inner_x, live, length, inner_p), hidden.astype(jnp.float32), params)
        grad_hidden, grad_params = pull(upstream.astype(jnp.float32))
        totals = tuple((left + right for left, right in zip(totals, grad_params)))
        return (totals, (result.astype(jnp.bfloat16), grad_hidden))
    zeros = tuple((jnp.zeros(param.shape, jnp.float32) for param in params))
    totals, (output, grad_tokens) = lax.scan(one_sequence, zeros, (tokens, cotangent, lengths, exit_layers))
    return (output, grad_tokens, totals[0], totals[1], totals[2], totals[3], totals[4], totals[5], totals[6], totals[7], totals[8], totals[9], totals[10], totals[11], totals[12], totals[13], totals[14])
```

```python
import jax
import jax.numpy as jnp
from jax import lax
from jax.experimental import pallas as pl
from jax.experimental.pallas import tpu as pltpu
from jax.sharding import Mesh
from jax.sharding import PartitionSpec as P

HEAD = 64
OWN = 128
MASKED = -1e30
LAST = (((1,), (1,)), ((), ()))


def block_at(info, place, rows=OWN):
    row, side = place // 2, place % 2
    return pl.multiple_of((lax.rem(row - info[0] + 4, 4) * 2 + lax.rem(side + info[1], 2)) * rows, rows)


def in_order(info, src, dst):
    for place in range(8):
        dst[place * OWN : (place + 1) * OWN, :] = src[pl.ds(block_at(info, place), OWN), :]


def head_of(values, head):
    lane = lax.broadcasted_iota(jnp.int32, values.shape, 1)
    return jnp.where(lane // HEAD == head, values, jnp.zeros_like(values))


def masked_scores(info, key_part, query_head, start):
    scores = lax.dot_general(key_part, query_head, LAST, preferred_element_type=jnp.float32)
    key_at = lax.broadcasted_iota(jnp.int32, scores.shape, 0)
    query_at = start + lax.broadcasted_iota(jnp.int32, (1, scores.shape[1]), 1)
    return jnp.where(key_at <= jnp.minimum(query_at, info[2] - 1), scores, MASKED)


def picked(rank_ref, place, rows):
    slot = lax.broadcasted_iota(jnp.int32, (rows, OWN), 0)
    return (slot == rank_ref[place : place + 1, :]).astype(jnp.float32).astype(jnp.bfloat16)


def forward_kernel(info, rank_ref, qkv_ref, ctx_ref, lse_ref, qkv, v_flip):
    rows = ctx_ref.shape[0] // 8
    in_order(info, qkv_ref, qkv)
    v_flip[...] = qkv[:, 256:384].T
    step = 2 * OWN
    for i in range(4):
        n = (i + 1) * step
        queries = qkv[i * step : n, 0:128]
        parts = []
        for head in range(2):
            scores = masked_scores(info, qkv[0:n, 128:256], head_of(queries, head), i * step)
            top = jnp.max(scores, 0, keepdims=True)
            weights = jnp.exp(scores - top)
            total = jnp.sum(weights, 0, keepdims=True)
            soft = (weights * (1.0 / total)).astype(jnp.bfloat16)
            parts.append(
                jnp.dot(v_flip[head * HEAD : (head + 1) * HEAD, 0:n], soft, preferred_element_type=jnp.float32)
            )
            lse_ref[0, head : head + 1, i * step : n] = top + jnp.log(total)
        block = jnp.concatenate(parts, 0).T.astype(jnp.bfloat16)
        for half in range(2):
            live = jnp.dot(
                picked(rank_ref, 2 * i + half, rows), block[half * OWN : (half + 1) * OWN], preferred_element_type=jnp.float32
            )
            ctx_ref[pl.ds(block_at(info, 2 * i + half, rows), rows), :] = live.astype(jnp.bfloat16)


def backward_kernel(info, rank_ref, qkv_ref, up_ref, lse_ref, out_ref, qkv, up, k_flip, dk, dv):
    rows = up_ref.shape[0] // 8
    in_order(info, qkv_ref, qkv)
    for place in range(8):
        live = lax.dot_general(
            picked(rank_ref, place, rows),
            up_ref[pl.ds(block_at(info, place, rows), rows), :],
            (((0,), (0,)), ((), ())),
            preferred_element_type=jnp.float32,
        )
        up[place * OWN : (place + 1) * OWN, :] = live.astype(jnp.bfloat16)
    k_flip[...] = qkv[:, 128:256].T
    step = 2 * OWN
    for i in (3, 2, 1, 0):
        n = (i + 1) * step
        queries = qkv[i * step : n, 0:128]
        upstream = up[i * step : n, :]
        parts = []
        for head in range(2):
            query_head = head_of(queries, head)
            up_head = head_of(upstream, head)
            scores = masked_scores(info, qkv[0:n, 128:256], query_head, i * step)
            soft = jnp.exp(scores - lse_ref[0, head : head + 1, i * step : n])
            value_part = jnp.dot(soft.astype(jnp.bfloat16), up_head, preferred_element_type=jnp.float32)
            grad_soft = lax.dot_general(qkv[0:n, 256:384], up_head, LAST, preferred_element_type=jnp.float32)
            weighted = jnp.sum(soft * grad_soft, 0, keepdims=True)
            grad_scores = (soft * (grad_soft - weighted)).astype(jnp.bfloat16)
            key_part = jnp.dot(grad_scores, query_head, preferred_element_type=jnp.float32)
            if i == 3 and head == 0:
                dv[...] = value_part
                dk[...] = key_part
            else:
                dv[0:n, :] += value_part
                dk[0:n, :] += key_part
            parts.append(
                jnp.dot(k_flip[head * HEAD : (head + 1) * HEAD, 0:n], grad_scores, preferred_element_type=jnp.float32)
            )
        block = jnp.concatenate(parts, 0).T.astype(jnp.bfloat16) * jnp.bfloat16(HEAD**-0.5)
        for half in range(2):
            out_ref[pl.ds(block_at(info, 2 * i + half), OWN), 0:128] = block[half * OWN : (half + 1) * OWN]
    for place in range(8):
        at = pl.ds(block_at(info, place), OWN)
        out_ref[at, 128:256] = dk[place * OWN : (place + 1) * OWN, :].astype(jnp.bfloat16)
        out_ref[at, 256:384] = dv[place * OWN : (place + 1) * OWN, :].astype(jnp.bfloat16)


def attend_forward(info, rank, qkv, slots):
    rows = qkv.shape[0]
    return pl.pallas_call(
        forward_kernel,
        grid=(2,),
        in_specs=[
            pl.BlockSpec(memory_space=pltpu.SMEM),
            pl.BlockSpec((8, OWN), lambda g: (0, 0)),
            pl.BlockSpec((rows, 384), lambda g: (0, g)),
        ],
        out_specs=[pl.BlockSpec((8 * slots, 128), lambda g: (0, g)), pl.BlockSpec((1, 8, rows), lambda g: (g, 0, 0))],
        out_shape=[jax.ShapeDtypeStruct((8 * slots, 256), jnp.bfloat16), jax.ShapeDtypeStruct((2, 8, rows), jnp.float32)],
        scratch_shapes=[pltpu.VMEM((rows, 384), jnp.bfloat16), pltpu.VMEM((128, rows), jnp.bfloat16)],
        compiler_params=pltpu.CompilerParams(vmem_limit_bytes=32 * 1024 * 1024),
        cost_estimate=pl.CostEstimate(flops=2 * 4 * rows * rows * 64 * 2, bytes_accessed=4 * 1024 * 1024, transcendentals=4 * rows * rows // 2),
        name="attend_forward",
    )(info, rank, qkv)


def attend_backward(info, rank, qkv, upstream, lse):
    rows = qkv.shape[0]
    return pl.pallas_call(
        backward_kernel,
        grid=(2,),
        in_specs=[
            pl.BlockSpec(memory_space=pltpu.SMEM),
            pl.BlockSpec((8, OWN), lambda g: (0, 0)),
            pl.BlockSpec((rows, 384), lambda g: (0, g)),
            pl.BlockSpec((upstream.shape[0], 128), lambda g: (0, g)),
            pl.BlockSpec((1, 8, rows), lambda g: (g, 0, 0)),
        ],
        out_specs=pl.BlockSpec((rows, 384), lambda g: (0, g)),
        out_shape=jax.ShapeDtypeStruct((rows, 768), jnp.bfloat16),
        scratch_shapes=[
            pltpu.VMEM((rows, 384), jnp.bfloat16),
            pltpu.VMEM((rows, 128), jnp.bfloat16),
            pltpu.VMEM((128, rows), jnp.bfloat16),
            pltpu.VMEM((rows, 128), jnp.float32),
            pltpu.VMEM((rows, 128), jnp.float32),
        ],
        compiler_params=pltpu.CompilerParams(vmem_limit_bytes=32 * 1024 * 1024),
        cost_estimate=pl.CostEstimate(flops=5 * 4 * rows * rows * 64 * 2, bytes_accessed=6 * 1024 * 1024, transcendentals=4 * rows * rows // 2),
        name="attend_backward",
    )(info, rank, qkv, upstream, lse)


LAYER = 12
FEW = 96
EPS = 1e-05
TP = ("y", "zl", "core")
DP = ("x", "zh")
EVERY = ("y", "zl", "core", "x", "zh")
SIDE = ("zl", "core", "zh")
UP = [(i, (i + 1) % 4) for i in range(4)]
DOWN = [(i, (i - 1) % 4) for i in range(4)]


def spot(z, core):
    return ((z % 2) * 2 + core) * 2 + z // 2


def away(z, core):
    return z if core == 0 else (4 - z) % 4


PARTNER = [(spot(z, c), spot(z ^ 1 if c == 0 else 3 - z, c)) for z in range(4) for c in range(2)]
CROSS = [(spot(z, 0), spot(away(z, 1), 1)) for z in range(4)] + [(spot(z, 1), spot(z, 0)) for z in range(4)]
BACK = [(b, a) for a, b in CROSS]
MOVE = [(spot(z, c), spot(away(z, c), c)) for z in range(4) for c in range(2)]


def f32(values):
    return values.astype(jnp.float32)


def bf16(values):
    return values.astype(jnp.bfloat16)


def after(values, earlier):
    return lax.optimization_barrier((values, earlier))[0]


def from_below(values):
    return lax.ppermute(values, "y", UP)


def from_above(values):
    return lax.ppermute(values, "y", DOWN)


def from_side(values):
    return lax.ppermute(values, SIDE, PARTNER)


def from_core(values):
    return lax.ppermute(values, "core", [(0, 1), (1, 0)])


def gather(own):
    rows = own.shape[0]
    half = rows // 2
    below, above, side = from_below(own), from_above(own), from_side(own)
    far = jnp.concatenate([from_below(below[:half]), from_above(above[half:])], 0)
    near_side = from_side(jnp.concatenate([below, above], 0))
    far_side = from_side(far)
    return [own, side, above, near_side[rows:], far, far_side, below, near_side[:rows]]


def scatter_sum(parts):
    rows = parts[0].shape[0]
    half = rows // 2
    far_side = from_side(parts[5])
    far = bf16(f32(parts[4]) + f32(far_side))
    near_side = from_side(after(jnp.concatenate([parts[7], parts[3]], 0), far_side))
    far_up, far_down = from_below(far[:half]), from_above(far[half:])
    below = f32(parts[6]) + f32(near_side[:rows])
    above = f32(parts[2]) + f32(near_side[rows:])
    to_above = bf16(jnp.concatenate([above[:half] + f32(far_up), above[half:]], 0))
    to_below = bf16(jnp.concatenate([below[:half], below[half:] + f32(far_down)], 0))
    own = f32(parts[0]) + f32(from_side(after(parts[1], near_side)))
    return own + f32(from_below(to_above)) + f32(from_above(to_below))


def products(left, right, dims=((1,), (0,))):
    rows = left.shape[0] // 8
    parts = [None] * 8
    for pair in (2, 3, 1, 0):
        block = left[pair * 2 * rows : (pair + 1) * 2 * rows]
        result = bf16(lax.dot_general(block, right, (dims, ((), ())), preferred_element_type=jnp.float32))
        parts[2 * pair], parts[2 * pair + 1] = result[:rows], result[rows:]
    return parts


def dp_summed(arrays):
    place, zh = lax.axis_index("x"), lax.axis_index("zh")
    rows = arrays[0].shape[0] // 4
    half = rows // 2

    def block(step):
        at = lax.rem(place + step, 4) * rows
        return jnp.concatenate([lax.dynamic_slice_in_dim(a, at, rows, 0) for a in arrays], 1)

    far, above, below, own = block(2), block(1), block(3), block(0)
    far_up = lax.ppermute(far[:half], "x", UP)
    far_down = lax.ppermute(far[half:], "x", DOWN)
    to_above = bf16(jnp.concatenate([f32(above[:half]) + f32(far_up), f32(above[half:])], 0))
    to_below = bf16(jnp.concatenate([f32(below[:half]), f32(below[half:]) + f32(far_down)], 0))
    total = f32(own) + f32(lax.ppermute(to_above, "x", UP)) + f32(lax.ppermute(to_below, "x", DOWN))
    mine = lax.dynamic_slice_in_dim(total, zh * half, half, 0)
    other = lax.dynamic_slice_in_dim(total, (1 - zh) * half, half, 0)
    return mine + f32(lax.ppermute(bf16(other), "zh", [(0, 1), (1, 0)]))


def norm_rows(values, gain, shift):
    average = jnp.mean(values, -1, keepdims=True)
    centred = values - average
    variance = jnp.mean(centred * centred, -1, keepdims=True)
    inverse = lax.rsqrt(variance + EPS)
    normed = centred * inverse
    return normed, inverse, normed * gain + shift


def norm_back(upstream, normed, inverse, gain):
    scaled = upstream * gain
    mean_term = jnp.mean(scaled, -1, keepdims=True)
    proj_term = jnp.mean(scaled * normed, -1, keepdims=True)
    return inverse * (scaled - mean_term - normed * proj_term)


def across(left, right):
    return lax.dot_general(left, right, (((0,), (0,)), ((), ())), preferred_element_type=jnp.float32)


def grad_summed(left, right_own, right_core):
    received = from_core(bf16(across(left, right_core)))
    return bf16(across(left, right_own) + f32(received))


def on_device(
    tokens,
    lengths,
    exit_layers,
    weight_query,
    bias_query,
    weight_key,
    weight_value,
    bias_value,
    weight_out,
    bias_out,
    weight_up,
    bias_up,
    weight_down,
    bias_down,
    gain_in,
    shift_in,
    gain_mid,
    shift_mid,
    cotangent,
):
    row, side, core = lax.axis_index("y"), lax.axis_index("zl"), lax.axis_index("core")
    dp_index = lax.axis_index("x") * 2 + lax.axis_index("zh")
    first_core = core == 0
    features = tokens.shape[-1]
    seq_len = exit_layers.shape[1]
    head_cols = weight_query.shape[1]
    hidden = weight_up.shape[1]
    own_rows = 2 * tokens.shape[1]

    def to_own(values):
        crossed = lax.ppermute(jnp.where(first_core, values[1], values[0]), SIDE, CROSS)
        moved = lax.ppermute(values[1], SIDE, MOVE)
        return jnp.concatenate(
            [jnp.where(first_core, values[0], crossed), jnp.where(first_core, crossed, moved)], 0
        )

    def to_home(values):
        first, second = values[: own_rows // 2], values[own_rows // 2 :]
        crossed = lax.ppermute(jnp.where(first_core, second, first), SIDE, BACK)
        moved = lax.ppermute(second, SIDE, MOVE)
        return jnp.stack([jnp.where(first_core, first, crossed), jnp.where(first_core, crossed, moved)], 0)

    tokens_low = to_own(tokens)
    tokens_own = f32(tokens_low)
    normed_in, inverse_in, normed_out = norm_rows(tokens_own, gain_in, shift_in)
    normed_out = bf16(normed_out)
    gathered_in = gather(normed_out)

    (
        exit_layers,
        lengths,
        cotangent,
        weight_query,
        weight_key,
        weight_value,
        weight_out,
        weight_up,
        weight_down,
        bias_query,
        bias_value,
        bias_up,
    ), _ = lax.optimization_barrier(
        (
            (
                exit_layers,
                lengths,
                cotangent,
                weight_query,
                weight_key,
                weight_value,
                weight_out,
                weight_up,
                weight_down,
                bias_query,
                bias_value,
                bias_up,
            ),
            normed_out,
        )
    )
    positions = jnp.arange(seq_len)
    live_pair = (positions[None, :] < lengths[:, None]) & (exit_layers >= LAYER)
    most = jnp.max(jnp.sum(live_pair.reshape(2, 8, own_rows).astype(jnp.int32), -1))
    most = jnp.max(lax.all_to_all(jnp.broadcast_to(most, (8, 128)), DP, 0, 0, tiled=True))

    about = jnp.concatenate([exit_layers[1], jnp.broadcast_to(lengths[1:], (128,))], 0)
    moved_about = lax.ppermute(about, SIDE, MOVE)
    exits = jnp.where(first_core, exit_layers[0], moved_about[:seq_len])
    length = jnp.where(first_core, lengths[0], moved_about[seq_len])
    live_all = ((positions < length) & (exits >= LAYER)).reshape(8, own_rows)
    upto = (jnp.arange(own_rows)[:, None] <= jnp.arange(own_rows)[None, :]).astype(jnp.bfloat16)
    counted = jnp.dot(live_all.astype(jnp.bfloat16), upto, preferred_element_type=jnp.float32)
    rank_all = jnp.where(live_all, counted.astype(jnp.int32) - 1, -1)
    place = row * 2 + side
    rank_own = lax.dynamic_slice_in_dim(rank_all, place, 1, 0)
    info = jnp.stack([row, side, length, jnp.int32(0)]).astype(jnp.int32)

    joined = jnp.concatenate([weight_query, weight_key, weight_value], 1)
    weight_qkv = jnp.concatenate([joined, from_core(joined)], 1)
    weight_out_chip = jnp.concatenate([weight_out, from_core(weight_out)], 0)
    weight_up_chip = jnp.concatenate([weight_up, from_core(weight_up)], 1)
    weight_down_chip = jnp.concatenate([weight_down, from_core(weight_down)], 0)
    biases = jnp.concatenate([bias_query, bias_value, bias_up])
    biases_core = from_core(biases)
    scale = HEAD**-0.5
    none = jnp.zeros((head_cols,), jnp.float32)
    bias_qkv = jnp.concatenate(
        [bias_query, none, bias_value, biases_core[:head_cols], none, biases_core[head_cols : 2 * head_cols]]
    )
    scale_qkv = jnp.tile(jnp.concatenate([none + scale, none + 1.0, none + 1.0]), 2)
    bias_up_chip = jnp.concatenate([bias_up, biases_core[2 * head_cols :]])
    cotangent_low = to_own(cotangent)
    hidden_in = jnp.concatenate(gathered_in, 0)
    width = 3 * head_cols
    part = features // 8

    def rest(slots, tokens_low, cotangent_low, normed_in, inverse_in, hidden_in, rank_all, rank_own, info, weight_qkv, weight_out_chip, weight_up_chip, weight_down_chip, bias_qkv, bias_up_chip):
        pick = (jnp.arange(slots)[:, None] == rank_own).astype(jnp.bfloat16)

        def take(values):
            return jnp.dot(pick, values, preferred_element_type=jnp.float32)

        def put(values, precision=None):
            return lax.dot_general(
                pick.astype(values.dtype),
                values,
                (((0,), (0,)), ((), ())),
                precision=precision,
                preferred_element_type=jnp.float32,
            )

        qkv = bf16((jnp.dot(hidden_in, weight_qkv, preferred_element_type=jnp.float32) + bias_qkv) * scale_qkv)
        grad_own = take(cotangent_low)
        grad_live = jnp.concatenate(gather(after(bf16(grad_own), qkv)), 0)
        context, lse = attend_forward(info, rank_all, qkv, slots)
        attention = scatter_sum(products(context, weight_out_chip))

        mid_own = take(tokens_low) + attention + bias_out
        normed_mid, inverse_mid, mid_out = norm_rows(mid_own, gain_mid, shift_mid)
        hidden_mid = jnp.concatenate(gather(bf16(mid_out)), 0)
        up_sum = jnp.dot(hidden_mid, weight_up_chip, preferred_element_type=jnp.float32) + bias_up_chip
        activated = bf16(jax.nn.gelu(up_sum))
        grad_activated = lax.dot_general(
            grad_live, weight_down_chip, (((1,), (1,)), ((), ())), preferred_element_type=jnp.float32
        )
        grad_up_sum = bf16(jax.vjp(jax.nn.gelu, up_sum)[1](grad_activated)[0])
        mid_grad = scatter_sum(products(grad_up_sum, weight_up_chip, ((1,), (1,))))
        back_step = norm_back(mid_grad, normed_mid, inverse_mid, gain_mid)
        back_own = grad_own + back_step
        back_low = jnp.concatenate(gather(bf16(back_own)), 0)

        branch = scatter_sum(after(products(activated, weight_down_chip), back_low))
        passed = pick.sum(0)[:, None] == 0
        out_rows = put(bf16(mid_own + branch + bias_down))
        output = to_home(bf16(jnp.where(passed, f32(tokens_low), out_rows)))

        grad_up = grad_summed(hidden_mid, grad_up_sum[:, :hidden], grad_up_sum[:, hidden:])
        grad_down = grad_summed(grad_live, activated[:, :hidden], activated[:, hidden:])
        summed_mlp = dp_summed([grad_up, grad_down])
        column_up = jnp.sum(f32(grad_up_sum), 0)
        shift_mid_part = jnp.sum(f32(weight_up_chip) * column_up, 1)
        gain_mid_part = jnp.sum(f32(grad_up) * f32(weight_up_chip[:, :hidden]), 1)

        grad_context = bf16(
            lax.dot_general(back_low, weight_out_chip, (((1,), (1,)), ((), ())), preferred_element_type=jnp.float32)
        )
        grad_qkv = attend_backward(info, rank_all, qkv, grad_context, lse)
        in_grad = scatter_sum(products(grad_qkv, weight_qkv, ((1,), (1,))))
        grad_in = grad_summed(hidden_in, grad_qkv[:, :width], grad_qkv[:, width:])
        grad_out = grad_summed(back_low, context[:, :head_cols], context[:, head_cols:])
        summed_attention = dp_summed([grad_in, grad_out])
        column_qkv = jnp.sum(f32(grad_qkv), 0)
        shift_in_part = jnp.sum(f32(weight_qkv) * column_qkv, 1)
        gain_in_part = jnp.sum(f32(grad_in) * f32(weight_qkv[:, :width]), 1)

        whole = [gain_in_part, shift_in_part, gain_mid_part, shift_mid_part, jnp.sum(back_own, 0), jnp.sum(grad_own, 0)]
        lines = [jnp.tile(w.reshape(8, part), (2, 1)) for w in whole]

        def by_core(mine, other):
            both = jnp.where(first_core, jnp.concatenate([mine, other]), jnp.concatenate([other, mine]))
            return both.reshape(16, -1)

        lines.append(by_core(column_up[:hidden], column_up[hidden:]))
        for begin in (0, 2 * head_cols):
            lines.append(
                by_core(column_qkv[begin : begin + head_cols], column_qkv[width + begin : width + begin + head_cols])
            )
        sent = jnp.concatenate(lines, 1)
        columns = sent.shape[1]
        sent = jnp.pad(sent, ((0, 0), (0, -columns % 128)))
        small = jnp.sum(lax.all_to_all(sent, ("core", "x", "zh"), 0, 0, tiled=True), 0)
        across_tp = jnp.broadcast_to(small[: 6 * part], (8, 6 * part))
        vectors = jnp.sum(lax.all_to_all(across_tp, ("y", "zl"), 0, 0, tiled=True), 0).reshape(6, part)
        at = 6 * part
        up_part = small[at : at + hidden // 8]
        at += hidden // 8
        query_part = small[at : at + head_cols // 8]
        at += head_cols // 8
        value_part = small[at : at + head_cols // 8]

        back_full = f32(cotangent_low) + put(back_step, lax.Precision.HIGHEST)
        grad_tokens = f32(to_home(bf16(back_full + norm_back(in_grad, normed_in, inverse_in, gain_in))))

        def of_dp(values):
            return lax.dynamic_slice_in_dim(values, dp_index * part, part, 0)

        return (
            output,
            grad_tokens,
            summed_attention[:, :head_cols],
            query_part,
            summed_attention[:, head_cols : 2 * head_cols],
            summed_attention[:, 2 * head_cols : width],
            value_part,
            summed_attention[:, width:].T,
            vectors[4],
            summed_mlp[:, :hidden],
            up_part,
            summed_mlp[:, hidden:].T,
            vectors[5],
            (vectors[0] - of_dp(shift_in) * vectors[1]) / of_dp(gain_in),
            vectors[1],
            (vectors[2] - of_dp(shift_mid) * vectors[3]) / of_dp(gain_mid),
            vectors[3],
        )

    state = (tokens_low, cotangent_low, normed_in, inverse_in, hidden_in, rank_all, rank_own, info, weight_qkv, weight_out_chip, weight_up_chip, weight_down_chip, bias_qkv, bias_up_chip)
    return lax.cond(most <= FEW, lambda *a: rest(FEW, *a), lambda *a: rest(own_rows, *a), *state)


def solution(mesh):
    names = Mesh(mesh.devices.reshape(4, 2, 2, 4, 2), EVERY)
    residual = P(DP, TP, None)
    return jax.shard_map(
        on_device,
        mesh=names,
        in_specs=(
            residual,
            P(DP),
            P(DP, None),
            P(None, TP),
            P(TP),
            P(None, TP),
            P(None, TP),
            P(TP),
            P(TP, None),
            P(),
            P(None, TP),
            P(TP),
            P(TP, None),
            P(),
            P(),
            P(),
            P(),
            P(),
            residual,
        ),
        out_specs=(
            residual,
            residual,
            P(DP, TP),
            P(EVERY),
            P(DP, TP),
            P(DP, TP),
            P(EVERY),
            P(TP, DP),
            P(DP),
            P(DP, TP),
            P(EVERY),
            P(TP, DP),
            P(DP),
            P(DP),
            P(DP),
            P(DP),
            P(DP),
        ),
        check_vma=False,
    )
```

```python
import jax
import jax.numpy as jnp
from jax import lax
from jax.experimental import pallas as pl
from jax.experimental.pallas import tpu as pltpu
from jax.experimental.layout import Layout, with_layout_constraint
from jax.sharding import Mesh
from jax.sharding import PartitionSpec as P

HEAD = 64
OWN = 128
MASKED = -1e30
LAST = (((1,), (1,)), ((), ()))


def block_at(info, place):
    step = lax.rem(info[3] * (place // 2 - info[0]) + 4, 4)
    side = lax.rem(place % 2 + info[1], 2)
    index = jnp.where(step == 1, 2, jnp.where(step == 2, 1, step))
    index = jnp.where(side == 0, index, jnp.where(index == 0, 7, 3 + index))
    return pl.multiple_of(index * OWN, OWN)


def in_order(info, src, dst):
    for place in range(8):
        dst[place * OWN : (place + 1) * OWN, :] = src[pl.ds(block_at(info, place), OWN), :]


def head_of(values, head):
    lane = lax.broadcasted_iota(jnp.int32, values.shape, 1)
    return jnp.where(lane // HEAD == head, values, jnp.zeros_like(values))


def masked_scores(info, key_part, query_head, start):
    scores = lax.dot_general(key_part, query_head, LAST, preferred_element_type=jnp.float32)
    key_at = lax.broadcasted_iota(jnp.int32, scores.shape, 0)
    query_at = start + lax.broadcasted_iota(jnp.int32, (1, scores.shape[1]), 1)
    return jnp.where(key_at <= jnp.minimum(query_at, info[2] - 1), scores, MASKED)


def forward_kernel(info, qkv_ref, ctx_ref, lse_ref, qkv, v_flip):
    in_order(info, qkv_ref, qkv)
    v_flip[...] = qkv[:, 256:384].T
    step = 2 * OWN
    for i in range(4):
        n = (i + 1) * step
        queries = qkv[i * step : n, 0:128]
        parts = []
        for head in range(2):
            scores = masked_scores(info, qkv[0:n, 128:256], head_of(queries, head), i * step)
            top = jnp.max(scores, 0, keepdims=True)
            weights = jnp.exp(scores - top)
            total = jnp.sum(weights, 0, keepdims=True)
            soft = (weights * (1.0 / total)).astype(jnp.bfloat16)
            parts.append(
                jnp.dot(v_flip[head * HEAD : (head + 1) * HEAD, 0:n], soft, preferred_element_type=jnp.float32)
            )
            lse_ref[0, head : head + 1, i * step : n] = top + jnp.log(total)
        block = jnp.concatenate(parts, 0).T.astype(jnp.bfloat16)
        for half in range(2):
            ctx_ref[pl.ds(block_at(info, 2 * i + half), OWN), :] = block[half * OWN : (half + 1) * OWN]


def backward_kernel(info, qkv_ref, up_ref, lse_ref, out_ref, qkv, up, k_flip, dk, dv):
    in_order(info, qkv_ref, qkv)
    in_order(info, up_ref, up)
    k_flip[...] = qkv[:, 128:256].T
    step = 2 * OWN
    for i in (3, 2, 1, 0):
        n = (i + 1) * step
        queries = qkv[i * step : n, 0:128]
        upstream = up[i * step : n, :]
        parts = []
        for head in range(2):
            query_head = head_of(queries, head)
            up_head = head_of(upstream, head)
            scores = masked_scores(info, qkv[0:n, 128:256], query_head, i * step)
            soft = jnp.exp(scores - lse_ref[0, head : head + 1, i * step : n])
            value_part = jnp.dot(soft.astype(jnp.bfloat16), up_head, preferred_element_type=jnp.float32)
            grad_soft = lax.dot_general(qkv[0:n, 256:384], up_head, LAST, preferred_element_type=jnp.float32)
            weighted = jnp.sum(soft * grad_soft, 0, keepdims=True)
            grad_scores = (soft * (grad_soft - weighted)).astype(jnp.bfloat16)
            key_part = jnp.dot(grad_scores, query_head, preferred_element_type=jnp.float32)
            if i == 3 and head == 0:
                dv[...] = value_part
                dk[...] = key_part
            else:
                dv[0:n, :] += value_part
                dk[0:n, :] += key_part
            parts.append(
                jnp.dot(k_flip[head * HEAD : (head + 1) * HEAD, 0:n], grad_scores, preferred_element_type=jnp.float32)
            )
        block = jnp.concatenate(parts, 0).T.astype(jnp.bfloat16) * jnp.bfloat16(HEAD**-0.5)
        for half in range(2):
            out_ref[pl.ds(block_at(info, 2 * i + half), OWN), 0:128] = block[half * OWN : (half + 1) * OWN]
    for place in range(8):
        at = pl.ds(block_at(info, place), OWN)
        out_ref[at, 128:256] = dk[place * OWN : (place + 1) * OWN, :].astype(jnp.bfloat16)
        out_ref[at, 256:384] = dv[place * OWN : (place + 1) * OWN, :].astype(jnp.bfloat16)


def attend_forward(info, qkv):
    rows = qkv.shape[0]
    return pl.pallas_call(
        forward_kernel,
        grid=(2,),
        in_specs=[pl.BlockSpec(memory_space=pltpu.SMEM), pl.BlockSpec((rows, 384), lambda g: (0, g))],
        out_specs=[pl.BlockSpec((rows, 128), lambda g: (0, g)), pl.BlockSpec((1, 8, rows), lambda g: (g, 0, 0))],
        out_shape=[
            jax.ShapeDtypeStruct((rows, 256), jnp.bfloat16),
            jax.ShapeDtypeStruct((2, 8, rows), jnp.float32),
        ],
        scratch_shapes=[pltpu.VMEM((rows, 384), jnp.bfloat16), pltpu.VMEM((128, rows), jnp.bfloat16)],
        compiler_params=pltpu.CompilerParams(vmem_limit_bytes=20 * 1024 * 1024),
        cost_estimate=pl.CostEstimate(
            flops=16 * rows * rows * HEAD, bytes_accessed=4 * 1024 * 1024, transcendentals=2 * rows * rows
        ),
        name="attend_forward",
    )(info, qkv)


def attend_backward(info, qkv, upstream, lse, pair):
    rows = qkv.shape[0]
    return pl.pallas_call(
        backward_kernel,
        grid=(1,),
        in_specs=[
            pl.BlockSpec(memory_space=pltpu.SMEM),
            pl.BlockSpec((rows, 384), lambda g: (0, pair)),
            pl.BlockSpec((rows, 128), lambda g: (0, pair)),
            pl.BlockSpec((1, 8, rows), lambda g: (pair, 0, 0)),
        ],
        out_specs=pl.BlockSpec((rows, 384), lambda g: (0, 0)),
        out_shape=jax.ShapeDtypeStruct((rows, 384), jnp.bfloat16),
        scratch_shapes=[
            pltpu.VMEM((rows, 384), jnp.bfloat16),
            pltpu.VMEM((rows, 128), jnp.bfloat16),
            pltpu.VMEM((128, rows), jnp.bfloat16),
            pltpu.VMEM((rows, 128), jnp.float32),
            pltpu.VMEM((rows, 128), jnp.float32),
        ],
        compiler_params=pltpu.CompilerParams(vmem_limit_bytes=20 * 1024 * 1024),
        cost_estimate=pl.CostEstimate(
            flops=20 * rows * rows * HEAD, bytes_accessed=3 * 1024 * 1024, transcendentals=rows * rows
        ),
        name="attend_backward",
    )(info, qkv, upstream, lse)


LAYER = 12
EPS = 1e-05
TP = ("y", "zl", "core")
DP = ("x", "zh")
EVERY = ("y", "zl", "core", "x", "zh")
SIDE = ("zl", "core", "zh")
AHEAD = [(i * 2 + c, ((i + 1 - 2 * c) % 4) * 2 + c) for i in range(4) for c in range(2)]
BEHIND = [(b, a) for a, b in AHEAD]
AHEAD_X = [(c * 4 + i, c * 4 + (i + 1 - 2 * c) % 4) for i in range(4) for c in range(2)]
BEHIND_X = [(b, a) for a, b in AHEAD_X]


def spot(z, core):
    return ((z % 2) * 2 + core) * 2 + z // 2


def away(z, core):
    return z if core == 0 else (4 - z) % 4


PARTNER = [(spot(z, c), spot(z ^ 1 if c == 0 else 3 - z, c)) for z in range(4) for c in range(2)]
CROSS = [(spot(z, 0), spot(away(z, 1), 1)) for z in range(4)] + [(spot(z, 1), spot(z, 0)) for z in range(4)]
BACK = [(b, a) for a, b in CROSS]
MOVE = [(spot(z, c), spot(away(z, c), c)) for z in range(4) for c in range(2)]


def f32(values):
    return values.astype(jnp.float32)


def bf16(values):
    return values.astype(jnp.bfloat16)


def after(values, *earlier):
    earlier = [e for e in earlier if e is not None]
    return lax.optimization_barrier((values, earlier))[0] if earlier else values


def from_behind(values, axis="y"):
    return lax.ppermute(values, (axis, "core") if axis == "y" else ("core", axis), AHEAD if axis == "y" else AHEAD_X)


def from_ahead(values, axis="y"):
    return lax.ppermute(values, (axis, "core") if axis == "y" else ("core", axis), BEHIND if axis == "y" else BEHIND_X)


def from_side(values):
    return lax.ppermute(values, SIDE, PARTNER)


def from_core(values):
    return lax.ppermute(values, "core", [(0, 1), (1, 0)])


class Gather:
    def __init__(self, own):
        self.own = own
        self.behind, self.ahead, self.side = from_behind(own), from_ahead(own), from_side(own)

    def second(self, *earlier):
        behind, ahead = after((self.behind, self.ahead), self.side, *earlier)
        self.far = from_behind(behind)
        self.ahead_side, self.behind_side = from_side(ahead), from_side(behind)
        self.near = behind
        return self

    def third(self, *earlier):
        self.far_side = from_side(after(self.far, self.ahead_side, self.behind_side, *earlier))
        return self

    def first_half(self, *earlier):
        return jnp.concatenate(after((self.own, self.far, self.ahead, self.behind), *earlier), 0)

    def second_half(self, *earlier):
        far_side = after(self.far_side, *earlier)
        return jnp.concatenate((far_side, self.ahead_side, self.behind_side, self.side), 0)


class ProductSum:
    def __init__(self, left, right, dims=((1,), (0,))):
        rest, sides = left
        self.count = rest.shape[0] // 4

        def times(block, earlier=None):
            block = after(block, earlier)
            return bf16(lax.dot_general(block, right, (dims, ((), ())), preferred_element_type=jnp.float32))

        count = self.count
        self.times, self.last = times, sides[3 * count :]
        self.first = times(sides[:count])
        self.near_part, self.rest = times(sides[count : 3 * count]), times(rest)

    def kept(self, index):
        return f32(self.rest[index * self.count : (index + 1) * self.count])

    def start(self, *earlier):
        self.far_side = from_side(after(self.first, *earlier))
        return self

    def second(self, *earlier):
        far_side = after(self.far_side, *earlier)
        self.side_part = self.times(self.last, far_side)
        self.near_side = from_side(after(self.near_part, far_side))
        self.far = from_behind(bf16(self.kept(1) + f32(far_side)))
        return self

    def third(self, *earlier):
        near_side, far = after((self.near_side, self.far), *earlier)
        count = self.count
        self.sent = (
            bf16(self.kept(3) + f32(near_side[count:])),
            bf16(self.kept(2) + f32(near_side[:count]) + f32(far)),
        )
        self.behind, self.ahead = from_ahead(self.sent[0]), from_behind(self.sent[1])
        self.own_side = from_side(after(self.side_part, near_side))
        return self

    def total(self, *earlier):
        own_side, behind, ahead = after((self.own_side, self.behind, self.ahead), *earlier)
        return self.kept(0) + f32(own_side) + f32(behind) + f32(ahead)


def halved(values):
    half = values.shape[0] // 2
    return values[:half], values[half:]


class DpSum:
    def __init__(self, arrays, sign):
        self.place, self.zh = lax.axis_index("x"), lax.axis_index("zh")
        count = arrays[0].shape[0] // 4

        def block(step):
            at = lax.rem(self.place + sign * step + 4, 4) * count
            return jnp.concatenate([lax.dynamic_slice_in_dim(a, at, count, 0) for a in arrays], 1)

        self.sent = (block(2), block(-1))
        self.far = from_behind(self.sent[0], "x")
        self.behind = from_ahead(self.sent[1], "x")
        self.to_ahead, self.own = block(1), block(0)

    def second(self, *earlier):
        far = after(self.far, *earlier)
        self.to_ahead = bf16(f32(self.to_ahead) + f32(far))
        self.ahead = from_behind(self.to_ahead, "x")
        return self

    def third(self, *earlier):
        behind, ahead = after((self.behind, self.ahead), *earlier)
        total = f32(self.own) + f32(behind) + f32(ahead)
        half = total.shape[0] // 2
        self.mine = lax.dynamic_slice_in_dim(total, self.zh * half, half, 0)
        other = lax.dynamic_slice_in_dim(total, (1 - self.zh) * half, half, 0)
        self.other = lax.ppermute(bf16(other), "zh", [(0, 1), (1, 0)])
        return self

    def total(self, *earlier):
        return self.mine + f32(after(self.other, *earlier))


def norm_rows(values, gain, shift):
    average = jnp.mean(values, -1, keepdims=True)
    centred = values - average
    variance = jnp.mean(centred * centred, -1, keepdims=True)
    inverse = lax.rsqrt(variance + EPS)
    normed = centred * inverse
    return normed, inverse, normed * gain + shift


def norm_back(upstream, normed, inverse, gain):
    scaled = upstream * gain
    mean_term = jnp.mean(scaled, -1, keepdims=True)
    proj_term = jnp.mean(scaled * normed, -1, keepdims=True)
    return inverse * (scaled - mean_term - normed * proj_term)


def across(left, right):
    return lax.dot_general(left, right, (((0,), (0,)), ((), ())), preferred_element_type=jnp.float32)


def times_columns(weights, columns):
    high = bf16(columns)
    pair = jnp.concatenate([high, bf16(columns - f32(high))], 0)
    product = lax.dot_general(pair, weights, (((1,), (1,)), ((), ())), preferred_element_type=jnp.float32)
    return jnp.sum(product, 0, keepdims=True)


def column_sums(values):
    return jnp.sum(f32(values), 0, keepdims=True)


class GradSum:
    def __init__(self, left, other):
        self.left = left
        self.sent = bf16(across(left, other))
        self.received = from_core(self.sent)

    def total(self, own, *earlier):
        left, own, received = after((self.left, own, self.received), *earlier)
        return bf16(across(left, own) + f32(received))


def on_device(
    tokens,
    lengths,
    exit_layers,
    weight_query,
    bias_query,
    weight_key,
    weight_value,
    bias_value,
    weight_out,
    bias_out,
    weight_up,
    bias_up,
    weight_down,
    bias_down,
    gain_in,
    shift_in,
    gain_mid,
    shift_mid,
    cotangent,
):
    row, side, core = lax.axis_index("y"), lax.axis_index("zl"), lax.axis_index("core")
    dp_index = lax.axis_index("x") * 2 + lax.axis_index("zh")
    tp_index = (row * 2 + side) * 2 + core
    first_core = core == 0
    features = tokens.shape[-1]
    seq_len = exit_layers.shape[1]
    head_cols = weight_query.shape[1]
    hidden = weight_up.shape[1]
    own_rows = 2 * tokens.shape[1]

    def to_own(values):
        crossed = lax.ppermute(jnp.where(first_core, values[1], values[0]), SIDE, CROSS)
        moved = lax.ppermute(values[1], SIDE, MOVE)
        return crossed, moved

    def owned(values, crossed, moved):
        return jnp.concatenate(
            [jnp.where(first_core, values[0], crossed), jnp.where(first_core, crossed, moved)], 0
        )

    def to_home(values):
        first, second = values[: own_rows // 2], values[own_rows // 2 :]
        crossed = lax.ppermute(jnp.where(first_core, second, first), SIDE, BACK)
        moved = lax.ppermute(second, SIDE, MOVE)
        return jnp.stack([jnp.where(first_core, first, crossed), jnp.where(first_core, crossed, moved)], 0)

    width = 3 * head_cols
    part = features // 8
    with jax.named_scope("own_rows"):
        tokens_own = f32(owned(tokens, *to_own(tokens)))
        normed_in, inverse_in, normed_out = norm_rows(tokens_own, gain_in, shift_in)
        normed_out = bf16(normed_out)
    with jax.named_scope("gather_in"):
        gathered_in = Gather(normed_out)
    with jax.named_scope("chip_weights"):
        biases = jnp.concatenate([bias_query, bias_value, bias_up])
        cotangent, exit_layers, lengths = after((cotangent, exit_layers, lengths), normed_out)
        weight_query, weight_key, weight_value = after((weight_query, weight_key, weight_value), gathered_in.side)
        joined = jnp.concatenate([weight_query, weight_key, weight_value], 1)
    with jax.named_scope("cotangent_rows"):
        cotangent_parts = to_own(cotangent)
        about = jnp.concatenate([exit_layers[1], jnp.broadcast_to(lengths[1:], (128,))], 0)
        moved_about = lax.ppermute(about, SIDE, MOVE)
    with jax.named_scope("gather_in"):
        gathered_in.second(joined)
    with jax.named_scope("chip_weights"):
        joined, weight_out, biases, weight_up, weight_down = after(
            (joined, weight_out, biases, weight_up, weight_down), gathered_in.near
        )
        joined_core = from_core(joined)
        weight_out_core, biases_core = from_core(weight_out), from_core(biases)
        weight_up_core, weight_down_core = from_core(weight_up), from_core(weight_down)
        weight_qkv = with_layout_constraint(
            jnp.concatenate(after([joined, joined_core], gathered_in.far), 1), Layout((0, 1))
        )

    with jax.named_scope("cotangent_rows"):
        cotangent_parts, moved_about = after((cotangent_parts, moved_about), gathered_in.far)
        cotangent_own = f32(owned(cotangent, *cotangent_parts))
        positions = jnp.arange(seq_len)
        exits = jnp.where(first_core, exit_layers[0], moved_about[:seq_len])
        length = jnp.where(first_core, lengths[0], moved_about[seq_len])
        live_all = f32((positions < length) & (exits >= LAYER))
        live_own = lax.dynamic_slice_in_dim(live_all, (row * 2 + side) * own_rows, own_rows, 0)[:, None]
        sign = 1 - 2 * core
        info = jnp.stack([row, side, length, sign]).astype(jnp.int32)
        grad_own = cotangent_own * live_own
        grad_own_low = bf16(grad_own)
    with jax.named_scope("gather_in"):
        gathered_in.third()
    with jax.named_scope("project"):
        first_in = gathered_in.first_half(weight_qkv, grad_own_low)
        scale = HEAD**-0.5
        none = jnp.zeros((head_cols,), jnp.float32)
        bias_qkv = jnp.concatenate(
            [biases[:head_cols], none, biases[head_cols : 2 * head_cols]]
            + [biases_core[:head_cols], none, biases_core[head_cols : 2 * head_cols]]
        )
        scale_qkv = jnp.tile(jnp.concatenate([none + scale, none + 1.0, none + 1.0]), 2)
        bias_up_chip = jnp.concatenate([biases[2 * head_cols :], biases_core[2 * head_cols :]])

        def projected(rows):
            product = jnp.dot(rows, weight_qkv, preferred_element_type=jnp.float32)
            return bf16((product + bias_qkv) * scale_qkv)

        first_qkv = projected(first_in)
        second_in = gathered_in.second_half(first_qkv)
        qkv = jnp.concatenate([first_qkv, projected(second_in)], 0)
        hidden_in = jnp.concatenate(after([first_in, second_in], qkv), 0)
    with jax.named_scope("chip_weights"):
        weight_out_chip = jnp.concatenate([weight_out, weight_out_core], 0)
        weight_out_chip, weight_up_core, weight_down_core = after(
            (weight_out_chip, weight_up_core, weight_down_core), gathered_in.far
        )
    with jax.named_scope("gather_cotangent"):
        gathered_grad = Gather(after(grad_own_low, qkv))
    context, lse = attend_forward(info, after(qkv, weight_out_chip, weight_up_core, weight_down_core))
    with jax.named_scope("sum_attention"):
        sum_att = ProductSum(halved(context), weight_out_chip).start().second()
    with jax.named_scope("chip_weights"):
        up_own, up_core, down_own, down_core = after(
            (weight_up, weight_up_core, weight_down, weight_down_core), sum_att.far_side
        )
        weight_up_chip = jnp.concatenate([up_own, up_core], 1)
        weight_down_chip = jnp.concatenate([down_own, down_core], 0)
    with jax.named_scope("sum_attention"):
        sum_att.third(weight_up_chip, weight_down_chip)
    with jax.named_scope("gather_cotangent"):
        gathered_grad.second(sum_att.far, sum_att.near_side)
    with jax.named_scope("sum_attention"):
        attention = sum_att.total()
    with jax.named_scope("gather_mid"):
        mid_own = tokens_own + live_own * (attention + bias_out)
        normed_mid, inverse_mid, mid_out = norm_rows(mid_own, gain_mid, shift_mid)
        mid_out = bf16(mid_out)
        gathered_mid = Gather(mid_out)
    with jax.named_scope("gather_cotangent"):
        gathered_grad.third(mid_out)
    with jax.named_scope("gather_mid"):
        gathered_mid.second()
    with jax.named_scope("feed_forward"):
        live_halves = (gathered_grad.first_half(gathered_mid.near), gathered_grad.second_half(gathered_mid.near))
        grad_activated = lax.optimization_barrier(
            [
                lax.dot_general(
                    half, weight_down_chip, (((1,), (1,)), ((), ())), preferred_element_type=jnp.float32
                )
                for half in live_halves
            ]
        )
    def fed(rows, upstream):
        up_sum = jnp.dot(rows, weight_up_chip, preferred_element_type=jnp.float32) + bias_up_chip
        return bf16(jax.nn.gelu(up_sum)), bf16(jax.vjp(jax.nn.gelu, up_sum)[1](upstream)[0])

    with jax.named_scope("feed_forward"):
        first_mid = gathered_mid.third().first_half(*grad_activated)
        first_fed = fed(first_mid, grad_activated[0])
        second_mid = gathered_mid.second_half(*first_fed)
        mid_halves = (first_mid, second_mid)
        activated, grad_up_sum = zip(first_fed, fed(second_mid, grad_activated[1]))
    with jax.named_scope("sum_mid_grad"):
        sum_mid = ProductSum(grad_up_sum, weight_up_chip, ((1,), (1,))).start().second()
    with jax.named_scope("feed_forward"):
        hidden_mid, grad_live, all_activated, all_grad_up = after(
            [jnp.concatenate(pair, 0) for pair in (mid_halves, live_halves, activated, grad_up_sum)], sum_mid.far_side
        )
    with jax.named_scope("sum_branch"):
        sum_branch = ProductSum(after(activated, sum_mid.far_side), weight_down_chip)
    with jax.named_scope("grads_mlp"):
        early_up, early_act = after((all_grad_up, all_activated), sum_mid.far, sum_mid.near_side)
        grads_up = GradSum(hidden_mid, early_up[:, hidden:])
        grads_down = GradSum(grad_live, early_act[:, hidden:])
    with jax.named_scope("sum_mid_grad"):
        sum_mid.third(sum_branch.first, sum_branch.near_part, sum_branch.rest)
        mid_grad = sum_mid.total(grads_up.sent, grads_down.sent)
    with jax.named_scope("sum_branch"):
        sum_branch.start(*sum_mid.sent)
    with jax.named_scope("gather_back"):
        back_own = cotangent_own + norm_back(mid_grad, normed_mid, inverse_mid, gain_mid)
        back_live = back_own * live_own
        back_low_own = bf16(back_live)
        gathered_back = Gather(back_low_own)
    with jax.named_scope("grads_mlp"):
        grad_up = grads_up.total(all_grad_up[:, :hidden], back_low_own)
        grad_down = grads_down.total(all_activated[:, :hidden], back_low_own)
    with jax.named_scope("gather_back"):
        gathered_back.second(grad_up, grad_down)
    with jax.named_scope("dp_mlp"):
        dp_mlp = DpSum(after([grad_up, grad_down], gathered_back.near), sign)
    with jax.named_scope("sum_branch"):
        sum_branch.second(gathered_back.near)
    with jax.named_scope("early_lines"):
        early_up = after(all_grad_up, gathered_back.far)
        early_vectors = after(
            [
                column_sums(mid_grad * normed_mid),
                column_sums(mid_grad),
                column_sums(back_live),
                column_sums(grad_own),
            ],
            gathered_back.far,
        )
        column_up = column_sums(early_up)
    with jax.named_scope("gather_back"):
        gathered_back.third(*dp_mlp.sent)
    with jax.named_scope("gather_back"):
        first_back = gathered_back.first_half()

    with jax.named_scope("grad_context"):

        def to_context(rows):
            product = lax.dot_general(
                rows, weight_out_chip, (((1,), (1,)), ((), ())), preferred_element_type=jnp.float32
            )
            return bf16(product)

        context_halves = halved(context)
        first_context = to_context(first_back)
        first_product = across(first_back, context_halves[0])
        second_back = gathered_back.second_half(first_context, first_product)
        grad_context = jnp.concatenate([first_context, to_context(second_back)], 0)
    with jax.named_scope("grads_attention"):
        product_out = first_product + across(after(second_back, grad_context), context_halves[1])
        product_own, product_core = product_out[:, :head_cols], bf16(product_out[:, head_cols:])
        received_out = from_core(product_core)
    grad_qkv_core = attend_backward(info, qkv, after(grad_context, product_own, product_core), lse, 1)
    with jax.named_scope("dp_mlp"):
        dp_mlp.second(grad_qkv_core)
    with jax.named_scope("sum_branch"):
        sum_branch.third(grad_context)
    with jax.named_scope("grads_attention"):
        grads_in = GradSum(hidden_in, grad_qkv_core)
        grad_out = bf16(product_own + f32(after(received_out, grad_qkv_core)))
        columns_core = column_sums(grad_qkv_core)
        shift_core = times_columns(weight_qkv[:, width:], columns_core)
    grad_qkv_own = attend_backward(
        info,
        qkv,
        after(grad_context, grads_in.received, grad_out, shift_core, column_up, early_vectors, dp_mlp.to_ahead, sum_branch.sent),
        lse,
        0,
    )
    with jax.named_scope("sum_in_grad"):
        grad_qkv = jnp.concatenate([grad_qkv_own, grad_qkv_core], 1)
        sum_in = ProductSum(halved(grad_qkv), weight_qkv, ((1,), (1,))).start()
    with jax.named_scope("sum_in_grad"):
        sum_in.second()
    with jax.named_scope("grads_attention"):
        grad_in = grads_in.total(grad_qkv_own, sum_in.side_part)
    with jax.named_scope("dp_attention"):
        dp_attention = DpSum([grad_in, grad_out], sign)
    with jax.named_scope("dp_mlp"):
        dp_mlp.third(sum_in.side_part)
    with jax.named_scope("sum_in_grad"):
        sum_in.third(*dp_attention.sent)
    with jax.named_scope("dp_attention"):
        dp_attention.second(*sum_in.sent)

    def of_dp(values):
        return lax.dynamic_slice_in_dim(values, dp_index * part, part, 0)

    with jax.named_scope("small_sums"):
        columns_own = column_sums(after(grad_qkv_own, *sum_in.sent))
        shift_in_part = shift_core + times_columns(weight_qkv[:, :width], columns_own)
        gain_in_part = jnp.sum(f32(after(grad_in, *sum_in.sent)) * f32(weight_qkv[:, :width]), 1)
        vectors = [v.reshape(8, part) for v in (shift_in_part, *early_vectors, gain_in_part)]
        sums = [column_up[:, :hidden], columns_own[:, :head_cols], columns_own[:, 2 * head_cols :]]
        sums += [column_up[:, hidden:], columns_core[:, :head_cols], columns_core[:, 2 * head_cols :]]
        lines = jnp.concatenate(vectors + [v.reshape(8, -1) for v in sums], 1)
        lines = after(jnp.pad(lines, ((0, 0), (0, -lines.shape[1] % 128))), dp_attention.to_ahead)
        small = jnp.sum(lax.all_to_all(lines, DP, 0, 0, tiled=True), 0)
    with jax.named_scope("sum_branch"):
        branch = sum_branch.total(*sum_in.sent)
        output_own = bf16(mid_own + live_own * (branch + bias_down))
    with jax.named_scope("sum_in_grad"):
        in_grad = sum_in.total(dp_attention.to_ahead, output_own)
    with jax.named_scope("dp_attention"):
        dp_attention.third(in_grad)
    with jax.named_scope("tokens_grad"):
        tokens_grad_own = bf16(back_own + norm_back(in_grad, normed_in, inverse_in, gain_in))
        grad_tokens = f32(to_home(tokens_grad_own))
    with jax.named_scope("sum_branch"):
        output = to_home(after(output_own, tokens_grad_own))
    with jax.named_scope("small_sums"):
        to_all = small[: 6 * part]
        wide, narrow = hidden // 8, head_cols // 8
        at = 6 * part + wide + 2 * narrow
        own_biases, side_biases = small[6 * part : at], small[at : at + wide + 2 * narrow]
        dest = jnp.arange(16)[:, None]
        for_biases = jnp.where(dest == tp_index, own_biases, jnp.where(dest == (tp_index ^ 1), side_biases, 0.0))
        sent = jnp.concatenate([jnp.broadcast_to(to_all, (16, 6 * part)), for_biases], 1)
        sent = after(jnp.pad(sent, ((0, 0), (0, -sent.shape[1] % 128))), tokens_grad_own)
        small = jnp.sum(lax.all_to_all(sent, TP, 0, 0, tiled=True), 0)
        vectors = small[: 6 * part].reshape(6, part)
        up_part, query_part, value_part = (
            small[6 * part + a : 6 * part + b]
            for a, b in ((0, wide), (wide, wide + narrow), (wide + narrow, wide + 2 * narrow))
        )

    with jax.named_scope("dp_attention"):
        summed_attention = dp_attention.total(tokens_grad_own)
    with jax.named_scope("dp_mlp"):
        summed_mlp = dp_mlp.total(tokens_grad_own)

    return (
        output,
        grad_tokens,
        summed_attention[:, :head_cols],
        query_part,
        summed_attention[:, head_cols : 2 * head_cols],
        summed_attention[:, 2 * head_cols : width],
        value_part,
        summed_attention[:, width : width + head_cols].T,
        vectors[3],
        summed_mlp[:, :hidden],
        up_part,
        summed_mlp[:, hidden:].T,
        vectors[4],
        (vectors[5] - of_dp(shift_in) * vectors[0]) / of_dp(gain_in),
        vectors[0],
        vectors[1],
        vectors[2],
    )


def solution(mesh):
    names = Mesh(mesh.devices.reshape(4, 2, 2, 4, 2), EVERY)
    residual = P(DP, TP, None)
    return jax.shard_map(
        on_device,
        mesh=names,
        in_specs=(
            residual,
            P(DP),
            P(DP, None),
            P(None, TP),
            P(TP),
            P(None, TP),
            P(None, TP),
            P(TP),
            P(TP, None),
            P(),
            P(None, TP),
            P(TP),
            P(TP, None),
            P(),
            P(),
            P(),
            P(),
            P(),
            residual,
        ),
        out_specs=(
            residual,
            residual,
            P(DP, TP),
            P(EVERY),
            P(DP, TP),
            P(DP, TP),
            P(EVERY),
            P(TP, DP),
            P(DP),
            P(DP, TP),
            P(EVERY),
            P(TP, DP),
            P(DP),
            P(DP),
            P(DP),
            P(DP),
            P(DP),
        ),
        check_vma=False,
    )
```

```python
import jax
import jax.numpy as jnp
from jax import lax
from jax.experimental import pallas as pl
from jax.experimental.pallas import tpu as pltpu
from jax.experimental.layout import Layout, with_layout_constraint
from jax.sharding import Mesh
from jax.sharding import PartitionSpec as P

HEAD = 64
OWN = 128
MASKED = -1e30
LAST = (((1,), (1,)), ((), ()))


def block_at(info, place):
    step = lax.rem(info[3] * (place // 2 - info[0]) + 4, 4)
    side = lax.rem(place % 2 + info[1], 2)
    index = jnp.where(step == 1, 2, jnp.where(step == 2, 1, step))
    index = jnp.where(side == 0, index, jnp.where(index == 0, 7, 3 + index))
    return pl.multiple_of(index * OWN, OWN)


def in_order(info, src, dst):
    for place in range(8):
        dst[place * OWN : (place + 1) * OWN, :] = src[pl.ds(block_at(info, place), OWN), :]


def head_of(values, head):
    lane = lax.broadcasted_iota(jnp.int32, values.shape, 1)
    return jnp.where(lane // HEAD == head, values, jnp.zeros_like(values))


def masked_scores(info, key_part, query_head, start):
    scores = lax.dot_general(key_part, query_head, LAST, preferred_element_type=jnp.float32)
    key_at = lax.broadcasted_iota(jnp.int32, scores.shape, 0)
    query_at = start + lax.broadcasted_iota(jnp.int32, (1, scores.shape[1]), 1)
    return jnp.where(key_at <= jnp.minimum(query_at, info[2] - 1), scores, MASKED)


def forward_kernel(info, qkv_ref, ctx_ref, lse_ref, qkv, v_flip):
    in_order(info, qkv_ref, qkv)
    v_flip[...] = qkv[:, 256:384].T
    step = 2 * OWN
    for i in range(4):
        n = (i + 1) * step
        queries = qkv[i * step : n, 0:128]
        parts = []
        for head in range(2):
            scores = masked_scores(info, qkv[0:n, 128:256], head_of(queries, head), i * step)
            top = jnp.max(scores, 0, keepdims=True)
            weights = jnp.exp(scores - top)
            total = jnp.sum(weights, 0, keepdims=True)
            product = jnp.dot(
                v_flip[head * HEAD : (head + 1) * HEAD, 0:n],
                weights.astype(jnp.bfloat16),
                preferred_element_type=jnp.float32,
            )
            parts.append(product * (1.0 / total))
            lse_ref[0, head : head + 1, i * step : n] = top + jnp.log(total)
        block = jnp.concatenate(parts, 0).T.astype(jnp.bfloat16)
        for half in range(2):
            ctx_ref[pl.ds(block_at(info, 2 * i + half), OWN), :] = block[half * OWN : (half + 1) * OWN]


def backward_kernel(info, qkv_ref, up_ref, lse_ref, out_ref, qkv, up, k_flip, dk, dv):
    in_order(info, qkv_ref, qkv)
    in_order(info, up_ref, up)
    k_flip[...] = qkv[:, 128:256].T
    step = 2 * OWN
    for i in (3, 2, 1, 0):
        n = (i + 1) * step
        queries = qkv[i * step : n, 0:128]
        upstream = up[i * step : n, :]
        parts = []
        for head in range(2):
            query_head = head_of(queries, head)
            up_head = head_of(upstream, head)
            scores = masked_scores(info, qkv[0:n, 128:256], query_head, i * step)
            soft = jnp.exp(scores - lse_ref[0, head : head + 1, i * step : n])
            value_part = jnp.dot(soft.astype(jnp.bfloat16), up_head, preferred_element_type=jnp.float32)
            grad_soft = lax.dot_general(qkv[0:n, 256:384], up_head, LAST, preferred_element_type=jnp.float32)
            weighted = jnp.sum(soft * grad_soft, 0, keepdims=True)
            grad_scores = (soft * (grad_soft - weighted)).astype(jnp.bfloat16)
            key_part = jnp.dot(grad_scores, query_head, preferred_element_type=jnp.float32)
            if i == 3 and head == 0:
                dv[...] = value_part
                dk[...] = key_part
            else:
                dv[0:n, :] += value_part
                dk[0:n, :] += key_part
            parts.append(
                jnp.dot(k_flip[head * HEAD : (head + 1) * HEAD, 0:n], grad_scores, preferred_element_type=jnp.float32)
            )
        block = jnp.concatenate(parts, 0).T.astype(jnp.bfloat16) * jnp.bfloat16(HEAD**-0.5)
        for half in range(2):
            out_ref[pl.ds(block_at(info, 2 * i + half), OWN), 0:128] = block[half * OWN : (half + 1) * OWN]
    for place in range(8):
        at = pl.ds(block_at(info, place), OWN)
        out_ref[at, 128:256] = dk[place * OWN : (place + 1) * OWN, :].astype(jnp.bfloat16)
        out_ref[at, 256:384] = dv[place * OWN : (place + 1) * OWN, :].astype(jnp.bfloat16)


def attend_forward(info, qkv):
    rows = qkv.shape[0]
    return pl.pallas_call(
        forward_kernel,
        grid=(2,),
        in_specs=[pl.BlockSpec(memory_space=pltpu.SMEM), pl.BlockSpec((rows, 384), lambda g: (0, g))],
        out_specs=[pl.BlockSpec((rows, 128), lambda g: (0, g)), pl.BlockSpec((1, 8, rows), lambda g: (g, 0, 0))],
        out_shape=[
            jax.ShapeDtypeStruct((rows, 256), jnp.bfloat16),
            jax.ShapeDtypeStruct((2, 8, rows), jnp.float32),
        ],
        scratch_shapes=[pltpu.VMEM((rows, 384), jnp.bfloat16), pltpu.VMEM((128, rows), jnp.bfloat16)],
        compiler_params=pltpu.CompilerParams(vmem_limit_bytes=20 * 1024 * 1024),
        cost_estimate=pl.CostEstimate(
            flops=16 * rows * rows * HEAD, bytes_accessed=4 * 1024 * 1024, transcendentals=2 * rows * rows
        ),
        name="attend_forward",
    )(info, qkv)


def attend_backward(info, qkv, upstream, lse, pair):
    rows = qkv.shape[0]
    return pl.pallas_call(
        backward_kernel,
        grid=(1,),
        in_specs=[
            pl.BlockSpec(memory_space=pltpu.SMEM),
            pl.BlockSpec((rows, 384), lambda g: (0, pair)),
            pl.BlockSpec((rows, 128), lambda g: (0, pair)),
            pl.BlockSpec((1, 8, rows), lambda g: (pair, 0, 0)),
        ],
        out_specs=pl.BlockSpec((rows, 384), lambda g: (0, 0)),
        out_shape=jax.ShapeDtypeStruct((rows, 384), jnp.bfloat16),
        scratch_shapes=[
            pltpu.VMEM((rows, 384), jnp.bfloat16),
            pltpu.VMEM((rows, 128), jnp.bfloat16),
            pltpu.VMEM((128, rows), jnp.bfloat16),
            pltpu.VMEM((rows, 128), jnp.float32),
            pltpu.VMEM((rows, 128), jnp.float32),
        ],
        compiler_params=pltpu.CompilerParams(vmem_limit_bytes=20 * 1024 * 1024),
        cost_estimate=pl.CostEstimate(
            flops=20 * rows * rows * HEAD, bytes_accessed=3 * 1024 * 1024, transcendentals=rows * rows
        ),
        name="attend_backward",
    )(info, qkv, upstream, lse)


LAYER = 12
EPS = 1e-05
TP = ("y", "zl", "core")
DP = ("x", "zh")
EVERY = ("y", "zl", "core", "x", "zh")
SIDE = ("zl", "core", "zh")
AHEAD = [(i * 2 + c, ((i + 1 - 2 * c) % 4) * 2 + c) for i in range(4) for c in range(2)]
BEHIND = [(b, a) for a, b in AHEAD]
AHEAD_X = [(c * 4 + i, c * 4 + (i + 1 - 2 * c) % 4) for i in range(4) for c in range(2)]
BEHIND_X = [(b, a) for a, b in AHEAD_X]


def spot(z, core):
    return ((z % 2) * 2 + core) * 2 + z // 2


def away(z, core):
    return z if core == 0 else (4 - z) % 4


PARTNER = [(spot(z, c), spot(z ^ 1 if c == 0 else 3 - z, c)) for z in range(4) for c in range(2)]
CROSS = [(spot(z, 0), spot(away(z, 1), 1)) for z in range(4)] + [(spot(z, 1), spot(z, 0)) for z in range(4)]
BACK = [(b, a) for a, b in CROSS]
MOVE = [(spot(z, c), spot(away(z, c), c)) for z in range(4) for c in range(2)]


def f32(values):
    return values.astype(jnp.float32)


def bf16(values):
    return values.astype(jnp.bfloat16)


def after(values, *earlier):
    earlier = [e for e in earlier if e is not None]
    return lax.optimization_barrier((values, earlier))[0] if earlier else values


def tied(values, *earlier):
    for array in earlier:
        values = values + 0.0 * f32(array[(slice(0, 1),) * array.ndim].reshape((1,) * values.ndim))
    return values


def from_behind(values, axis="y"):
    return lax.ppermute(values, (axis, "core") if axis == "y" else ("core", axis), AHEAD if axis == "y" else AHEAD_X)


def from_ahead(values, axis="y"):
    return lax.ppermute(values, (axis, "core") if axis == "y" else ("core", axis), BEHIND if axis == "y" else BEHIND_X)


def from_side(values):
    return lax.ppermute(values, SIDE, PARTNER)


def from_core(values):
    return lax.ppermute(values, "core", [(0, 1), (1, 0)])


class Gather:
    def __init__(self, own):
        self.own = own
        self.behind, self.ahead, self.side = from_behind(own), from_ahead(own), from_side(own)

    def second(self, *earlier):
        behind, ahead = after((self.behind, self.ahead), self.side, *earlier)
        self.far = from_behind(behind)
        self.ahead_side, self.behind_side = from_side(ahead), from_side(behind)
        self.near = behind
        return self

    def third(self, *earlier):
        self.far_side = from_side(after(self.far, self.ahead_side, self.behind_side, *earlier))
        return self

    def first_half(self, *earlier):
        return jnp.concatenate(after((self.own, self.far, self.ahead, self.behind), *earlier), 0)

    def second_half(self, *earlier):
        far_side = after(self.far_side, *earlier)
        return jnp.concatenate((far_side, self.ahead_side, self.behind_side, self.side), 0)


class ProductSum:
    def __init__(self, left, right, dims=((1,), (0,))):
        rest, sides = left
        self.count = rest.shape[0] // 4

        def times(block, earlier=None):
            block = after(block, earlier)
            return bf16(lax.dot_general(block, right, (dims, ((), ())), preferred_element_type=jnp.float32))

        count = self.count
        self.times, self.last = times, sides[3 * count :]
        self.first = times(sides[:count])
        self.near_part, self.rest = times(sides[count : 3 * count]), times(rest)

    def kept(self, index):
        return f32(self.rest[index * self.count : (index + 1) * self.count])

    def start(self, *earlier):
        self.far_side = from_side(after(self.first, *earlier))
        return self

    def second(self, *earlier):
        far_side = after(self.far_side, *earlier)
        self.side_part = self.times(self.last, far_side)
        self.near_side = from_side(after(self.near_part, far_side))
        self.far = from_behind(bf16(self.kept(1) + f32(far_side)))
        return self

    def third(self, *earlier):
        near_side, far = after((self.near_side, self.far), *earlier)
        count = self.count
        self.sent = (
            bf16(self.kept(3) + f32(near_side[count:])),
            bf16(self.kept(2) + f32(near_side[:count]) + f32(far)),
        )
        self.behind, self.ahead = from_ahead(self.sent[0]), from_behind(self.sent[1])
        self.own_side = from_side(after(self.side_part, near_side))
        return self

    def total(self, *earlier):
        own_side, behind, ahead = after((self.own_side, self.behind, self.ahead), *earlier)
        return self.kept(0) + f32(own_side) + f32(behind) + f32(ahead)


def halved(values):
    half = values.shape[0] // 2
    return values[:half], values[half:]


class DpSum:
    def __init__(self, arrays, sign):
        self.place, self.zh = lax.axis_index("x"), lax.axis_index("zh")
        count = arrays[0].shape[0] // 4

        def block(step):
            at = lax.rem(self.place + sign * step + 4, 4) * count
            return jnp.concatenate([lax.dynamic_slice_in_dim(a, at, count, 0) for a in arrays], 1)

        self.sent = (block(2), block(-1))
        self.far = from_behind(self.sent[0], "x")
        self.behind = from_ahead(self.sent[1], "x")
        self.to_ahead, self.own = block(1), block(0)

    def second(self, *earlier):
        far = after(self.far, *earlier)
        self.to_ahead = bf16(f32(self.to_ahead) + f32(far))
        self.ahead = from_behind(self.to_ahead, "x")
        return self

    def third(self, *earlier):
        behind, ahead = after((self.behind, self.ahead), *earlier)
        total = f32(self.own) + f32(behind) + f32(ahead)
        half = total.shape[0] // 2
        self.mine = lax.dynamic_slice_in_dim(total, self.zh * half, half, 0)
        other = lax.dynamic_slice_in_dim(total, (1 - self.zh) * half, half, 0)
        self.other = lax.ppermute(bf16(other), "zh", [(0, 1), (1, 0)])
        return self

    def total(self, *earlier):
        return self.mine + f32(after(self.other, *earlier))


def norm_rows(values, gain, shift):
    average = jnp.mean(values, -1, keepdims=True)
    centred = values - average
    variance = jnp.mean(centred * centred, -1, keepdims=True)
    inverse = lax.rsqrt(variance + EPS)
    normed = centred * inverse
    return normed, inverse, normed * gain + shift


def norm_back(upstream, normed, inverse, gain):
    scaled = upstream * gain
    mean_term = jnp.mean(scaled, -1, keepdims=True)
    proj_term = jnp.mean(scaled * normed, -1, keepdims=True)
    return inverse * (scaled - mean_term - normed * proj_term)


def across(left, right):
    return lax.dot_general(left, right, (((0,), (0,)), ((), ())), preferred_element_type=jnp.float32)


def times_columns(weights, columns):
    high = bf16(columns)
    pair = jnp.concatenate([high, bf16(columns - f32(high))], 0)
    product = lax.dot_general(pair, weights, (((1,), (1,)), ((), ())), preferred_element_type=jnp.float32)
    return jnp.sum(product, 0, keepdims=True)


def column_sums(values):
    return jnp.sum(f32(values), 0, keepdims=True)


class GradSum:
    def __init__(self, left, other):
        self.left = left
        self.sent = bf16(across(left, other))
        self.received = from_core(self.sent)

    def total(self, own, *earlier):
        left, own, received = after((self.left, own, self.received), *earlier)
        return bf16(across(left, own) + f32(received))


def on_device(
    tokens,
    lengths,
    exit_layers,
    weight_query,
    bias_query,
    weight_key,
    weight_value,
    bias_value,
    weight_out,
    bias_out,
    weight_up,
    bias_up,
    weight_down,
    bias_down,
    gain_in,
    shift_in,
    gain_mid,
    shift_mid,
    cotangent,
):
    row, side, core = lax.axis_index("y"), lax.axis_index("zl"), lax.axis_index("core")
    dp_index = lax.axis_index("x") * 2 + lax.axis_index("zh")
    tp_index = (row * 2 + side) * 2 + core
    first_core = core == 0
    features = tokens.shape[-1]
    seq_len = exit_layers.shape[1]
    head_cols = weight_query.shape[1]
    hidden = weight_up.shape[1]
    own_rows = 2 * tokens.shape[1]

    def to_own(values):
        crossed = lax.ppermute(jnp.where(first_core, values[1], values[0]), SIDE, CROSS)
        moved = lax.ppermute(values[1], SIDE, MOVE)
        return crossed, moved

    def owned(values, crossed, moved):
        return jnp.concatenate(
            [jnp.where(first_core, values[0], crossed), jnp.where(first_core, crossed, moved)], 0
        )

    def to_home(values):
        first, second = values[: own_rows // 2], values[own_rows // 2 :]
        crossed = lax.ppermute(jnp.where(first_core, second, first), SIDE, BACK)
        moved = lax.ppermute(second, SIDE, MOVE)
        return jnp.stack([jnp.where(first_core, first, crossed), jnp.where(first_core, crossed, moved)], 0)

    width = 3 * head_cols
    part = features // 8
    with jax.named_scope("own_rows"):
        tokens_own = f32(owned(tokens, *to_own(tokens)))
        normed_in, inverse_in, normed_out = norm_rows(tokens_own, gain_in, shift_in)
        normed_out = bf16(normed_out)
    with jax.named_scope("gather_in"):
        gathered_in = Gather(normed_out)
    with jax.named_scope("chip_weights"):
        biases = jnp.concatenate([bias_query, bias_value, bias_up])
        cotangent, exit_layers, lengths = after((cotangent, exit_layers, lengths), normed_out)
        weight_query, weight_key, weight_value = after((weight_query, weight_key, weight_value), gathered_in.side)
        joined = jnp.concatenate([weight_query, weight_key, weight_value], 1)
    with jax.named_scope("cotangent_rows"):
        cotangent_parts = to_own(cotangent)
        about = jnp.concatenate([exit_layers[1], jnp.broadcast_to(lengths[1:], (128,))], 0)
        moved_about = lax.ppermute(about, SIDE, MOVE)
    with jax.named_scope("gather_in"):
        gathered_in.second(joined)
    with jax.named_scope("chip_weights"):
        joined, weight_out, biases, weight_up, weight_down = after(
            (joined, weight_out, biases, weight_up, weight_down), gathered_in.near
        )
        joined_core = from_core(joined)
        weight_out_core, biases_core = from_core(weight_out), from_core(biases)
        weight_up_core, weight_down_core = from_core(weight_up), from_core(weight_down)
        weight_qkv = with_layout_constraint(
            jnp.concatenate(after([joined, joined_core], gathered_in.far), 1), Layout((0, 1))
        )

    with jax.named_scope("cotangent_rows"):
        cotangent_parts, moved_about = after((cotangent_parts, moved_about), gathered_in.far)
        cotangent_own = f32(owned(cotangent, *cotangent_parts))
        positions = jnp.arange(seq_len)
        exits = jnp.where(first_core, exit_layers[0], moved_about[:seq_len])
        length = jnp.where(first_core, lengths[0], moved_about[seq_len])
        live_all = f32((positions < length) & (exits >= LAYER))
        live_own = lax.dynamic_slice_in_dim(live_all, (row * 2 + side) * own_rows, own_rows, 0)[:, None]
        sign = 1 - 2 * core
        info = jnp.stack([row, side, length, sign]).astype(jnp.int32)
        grad_own = cotangent_own * live_own
        grad_own_low = bf16(grad_own)
    with jax.named_scope("gather_in"):
        gathered_in.third()
    with jax.named_scope("project"):
        first_in = gathered_in.first_half(weight_qkv, grad_own_low)
        scale = HEAD**-0.5
        none = jnp.zeros((head_cols,), jnp.float32)
        bias_qkv = jnp.concatenate(
            [biases[:head_cols], none, biases[head_cols : 2 * head_cols]]
            + [biases_core[:head_cols], none, biases_core[head_cols : 2 * head_cols]]
        )
        scale_qkv = jnp.tile(jnp.concatenate([none + scale, none + 1.0, none + 1.0]), 2)
        bias_up_chip = jnp.concatenate([biases[2 * head_cols :], biases_core[2 * head_cols :]])

        def projected(rows):
            product = jnp.dot(rows, weight_qkv, preferred_element_type=jnp.float32)
            return bf16((product + bias_qkv) * scale_qkv)

        first_qkv = projected(first_in)
        second_in = gathered_in.second_half(first_qkv)
        qkv = jnp.concatenate([first_qkv, projected(second_in)], 0)
        hidden_in = jnp.concatenate(after([first_in, second_in], qkv), 0)
    with jax.named_scope("chip_weights"):
        weight_out_chip = jnp.concatenate([weight_out, weight_out_core], 0)
        weight_out_chip, weight_up_core, weight_down_core = after(
            (weight_out_chip, weight_up_core, weight_down_core), gathered_in.far
        )
    with jax.named_scope("gather_cotangent"):
        gathered_grad = Gather(after(grad_own_low, qkv))
    context, lse = attend_forward(info, after(qkv, weight_out_chip, weight_up_core, weight_down_core))
    with jax.named_scope("sum_attention"):
        sum_att = ProductSum(halved(context), weight_out_chip).start().second()
    with jax.named_scope("chip_weights"):
        up_own, up_core, down_own, down_core = after(
            (weight_up, weight_up_core, weight_down, weight_down_core), sum_att.far_side
        )
        weight_up_chip = jnp.concatenate([up_own, up_core], 1)
        weight_down_chip = jnp.concatenate([down_own, down_core], 0)
    with jax.named_scope("sum_attention"):
        sum_att.third(weight_up_chip, weight_down_chip)
    with jax.named_scope("gather_cotangent"):
        gathered_grad.second(sum_att.far, sum_att.near_side)
    with jax.named_scope("sum_attention"):
        attention = sum_att.total()
    with jax.named_scope("gather_mid"):
        mid_own = tokens_own + live_own * (attention + bias_out)
        normed_mid, inverse_mid, mid_out = norm_rows(mid_own, gain_mid, shift_mid)
        mid_out = bf16(mid_out)
        gathered_mid = Gather(mid_out)
    with jax.named_scope("gather_cotangent"):
        gathered_grad.third(mid_out)
    with jax.named_scope("gather_mid"):
        gathered_mid.second()
    with jax.named_scope("feed_forward"):
        live_halves = (gathered_grad.first_half(gathered_mid.near), gathered_grad.second_half(gathered_mid.near))
        grad_activated = lax.optimization_barrier(
            [
                lax.dot_general(
                    half, weight_down_chip, (((1,), (1,)), ((), ())), preferred_element_type=jnp.float32
                )
                for half in live_halves
            ]
        )
    def fed(rows, upstream):
        up_sum = jnp.dot(rows, weight_up_chip, preferred_element_type=jnp.float32) + bias_up_chip
        return bf16(jax.nn.gelu(up_sum)), bf16(jax.vjp(jax.nn.gelu, up_sum)[1](upstream)[0])

    with jax.named_scope("feed_forward"):
        first_mid = gathered_mid.third().first_half(*grad_activated)
        first_fed = fed(first_mid, grad_activated[0])
        second_mid = gathered_mid.second_half(*first_fed)
        mid_halves = (first_mid, second_mid)
        activated, grad_up_sum = zip(first_fed, fed(second_mid, grad_activated[1]))
    with jax.named_scope("sum_mid_grad"):
        sum_mid = ProductSum(grad_up_sum, weight_up_chip, ((1,), (1,))).start().second()
    with jax.named_scope("feed_forward"):
        hidden_mid, grad_live, all_activated, all_grad_up = after(
            [jnp.concatenate(pair, 0) for pair in (mid_halves, live_halves, activated, grad_up_sum)], sum_mid.far_side
        )
    with jax.named_scope("sum_branch"):
        sum_branch = ProductSum(after(activated, sum_mid.far_side), weight_down_chip)
    with jax.named_scope("grads_mlp"):
        early_up, early_act = after((all_grad_up, all_activated), sum_mid.far, sum_mid.near_side)
        grads_up = GradSum(hidden_mid, early_up[:, hidden:])
        grads_down = GradSum(grad_live, early_act[:, hidden:])
    with jax.named_scope("sum_mid_grad"):
        sum_mid.third(sum_branch.first, sum_branch.near_part, sum_branch.rest)
        mid_grad = sum_mid.total(grads_up.sent, grads_down.sent)
    with jax.named_scope("sum_branch"):
        sum_branch.start(*sum_mid.sent)
    with jax.named_scope("gather_back"):
        back_own = cotangent_own + norm_back(mid_grad, normed_mid, inverse_mid, gain_mid)
        back_live = back_own * live_own
        back_low_own = bf16(back_live)
        gathered_back = Gather(back_low_own)
    with jax.named_scope("grads_mlp"):
        grad_up = grads_up.total(all_grad_up[:, :hidden], back_low_own)
        grad_down = grads_down.total(all_activated[:, :hidden], back_low_own)
    with jax.named_scope("gather_back"):
        gathered_back.second(grad_up, grad_down)
    with jax.named_scope("dp_mlp"):
        dp_mlp = DpSum(after([grad_up, grad_down], gathered_back.near), sign)
    with jax.named_scope("sum_branch"):
        sum_branch.second(gathered_back.near)
    with jax.named_scope("early_lines"):
        early_up = after(all_grad_up, gathered_back.far)
        early_vectors = after(
            [
                column_sums(mid_grad * normed_mid),
                column_sums(mid_grad),
                column_sums(back_live),
                column_sums(grad_own),
            ],
            gathered_back.far,
        )
        column_up = column_sums(early_up)
    with jax.named_scope("gather_back"):
        gathered_back.third(*dp_mlp.sent)
    with jax.named_scope("gather_back"):
        first_back = gathered_back.first_half()

    with jax.named_scope("grad_context"):

        def to_context(rows):
            product = lax.dot_general(
                rows, weight_out_chip, (((1,), (1,)), ((), ())), preferred_element_type=jnp.float32
            )
            return bf16(product)

        context_halves = halved(context)
        first_context = to_context(first_back)
        first_product = across(first_back, context_halves[0])
        second_back = gathered_back.second_half(first_context, first_product)
        grad_context = jnp.concatenate([first_context, to_context(second_back)], 0)
    with jax.named_scope("grads_attention"):
        product_out = first_product + across(after(second_back, grad_context), context_halves[1])
        product_own, product_core = product_out[:, :head_cols], bf16(product_out[:, head_cols:])
        received_out = from_core(product_core)
    grad_qkv_core = attend_backward(info, qkv, after(grad_context, product_own, product_core), lse, 1)
    with jax.named_scope("dp_mlp"):
        dp_mlp.second(grad_qkv_core)
    with jax.named_scope("sum_branch"):
        sum_branch.third(grad_context)
    with jax.named_scope("grads_attention"):
        grads_in = GradSum(hidden_in, grad_qkv_core)
        grad_out = bf16(product_own + f32(after(received_out, grad_qkv_core)))
        columns_core = column_sums(grad_qkv_core)
        shift_core = times_columns(weight_qkv[:, width:], columns_core)
    grad_qkv_own = attend_backward(
        info,
        qkv,
        after(grad_context, grads_in.received, grad_out, shift_core, column_up, early_vectors, dp_mlp.to_ahead, sum_branch.sent),
        lse,
        0,
    )
    with jax.named_scope("sum_in_grad"):
        grad_qkv = jnp.concatenate([grad_qkv_own, grad_qkv_core], 1)
        sum_in = ProductSum(halved(grad_qkv), weight_qkv, ((1,), (1,))).start()
    with jax.named_scope("sum_in_grad"):
        sum_in.second()
    with jax.named_scope("grads_attention"):
        grad_in = grads_in.total(grad_qkv_own, sum_in.side_part)
    with jax.named_scope("dp_attention"):
        dp_attention = DpSum([grad_in, grad_out], sign)
    with jax.named_scope("dp_mlp"):
        dp_mlp.third(sum_in.side_part)
    with jax.named_scope("sum_in_grad"):
        sum_in.third(*dp_attention.sent)
    with jax.named_scope("dp_attention"):
        dp_attention.second(*sum_in.sent)

    def of_dp(values):
        return lax.dynamic_slice_in_dim(values, dp_index * part, part, 0)

    with jax.named_scope("small_sums"):
        columns_own = column_sums(after(grad_qkv_own, *sum_in.sent))
        shift_in_part = shift_core + times_columns(weight_qkv[:, :width], columns_own)
        gain_in_part = jnp.sum(f32(after(grad_in, *sum_in.sent)) * f32(weight_qkv[:, :width]), 1)
        vectors = [v.reshape(8, part) for v in (shift_in_part, *early_vectors, gain_in_part)]
        sums = [column_up[:, :hidden], columns_own[:, :head_cols], columns_own[:, 2 * head_cols :]]
        sums += [column_up[:, hidden:], columns_core[:, :head_cols], columns_core[:, 2 * head_cols :]]
        lines = jnp.concatenate(vectors + [v.reshape(8, -1) for v in sums], 1)
        lines = after(jnp.pad(lines, ((0, 0), (0, -lines.shape[1] % 128))), dp_attention.to_ahead)
        small = jnp.sum(lax.all_to_all(lines, DP, 0, 0, tiled=True), 0)
    with jax.named_scope("sum_branch"):
        branch = sum_branch.total(*sum_in.sent)
        output_own = bf16(mid_own + live_own * (branch + bias_down))
    with jax.named_scope("sum_in_grad"):
        in_grad = tied(sum_in.total(dp_attention.to_ahead, output_own), dp_attention.ahead)
    with jax.named_scope("dp_attention"):
        dp_attention.third(in_grad)
    with jax.named_scope("tokens_grad"):
        tokens_grad_own = bf16(back_own + norm_back(in_grad, normed_in, inverse_in, gain_in))
        tokens_grad_home = to_home(tokens_grad_own)
        grad_tokens = f32(tokens_grad_home)
    with jax.named_scope("sum_branch"):
        output = to_home(after(output_own, tokens_grad_own))
    with jax.named_scope("small_sums"):
        to_all = small[: 6 * part]
        wide, narrow = hidden // 8, head_cols // 8
        at = 6 * part + wide + 2 * narrow
        own_biases, side_biases = small[6 * part : at], small[at : at + wide + 2 * narrow]
        dest = jnp.arange(16)[:, None]
        for_biases = jnp.where(dest == tp_index, own_biases, jnp.where(dest == (tp_index ^ 1), side_biases, 0.0))
        sent = jnp.concatenate([jnp.broadcast_to(to_all, (16, 6 * part)), for_biases], 1)
        sent = tied(jnp.pad(sent, ((0, 0), (0, -sent.shape[1] % 128))), tokens_grad_home[1])
        small = jnp.sum(lax.all_to_all(sent, TP, 0, 0, tiled=True), 0)
        vectors = small[: 6 * part].reshape(6, part)
        up_part, query_part, value_part = (
            small[6 * part + a : 6 * part + b]
            for a, b in ((0, wide), (wide, wide + narrow), (wide + narrow, wide + 2 * narrow))
        )

    with jax.named_scope("dp_attention"):
        summed_attention = dp_attention.total(tokens_grad_own)
    with jax.named_scope("dp_mlp"):
        summed_mlp = tied(dp_mlp.total(), tokens_grad_home[1])

    return (
        output,
        grad_tokens,
        summed_attention[:, :head_cols],
        query_part,
        summed_attention[:, head_cols : 2 * head_cols],
        summed_attention[:, 2 * head_cols : width],
        value_part,
        summed_attention[:, width : width + head_cols].T,
        vectors[3],
        summed_mlp[:, :hidden],
        up_part,
        summed_mlp[:, hidden:].T,
        vectors[4],
        (vectors[5] - of_dp(shift_in) * vectors[0]) / of_dp(gain_in),
        vectors[0],
        vectors[1],
        vectors[2],
    )


def solution(mesh):
    names = Mesh(mesh.devices.reshape(4, 2, 2, 4, 2), EVERY)
    residual = P(DP, TP, None)
    return jax.shard_map(
        on_device,
        mesh=names,
        in_specs=(
            residual,
            P(DP),
            P(DP, None),
            P(None, TP),
            P(TP),
            P(None, TP),
            P(None, TP),
            P(TP),
            P(TP, None),
            P(),
            P(None, TP),
            P(TP),
            P(TP, None),
            P(),
            P(),
            P(),
            P(),
            P(),
            residual,
        ),
        out_specs=(
            residual,
            residual,
            P(DP, TP),
            P(EVERY),
            P(DP, TP),
            P(DP, TP),
            P(EVERY),
            P(TP, DP),
            P(DP),
            P(DP, TP),
            P(EVERY),
            P(TP, DP),
            P(DP),
            P(DP),
            P(DP),
            P(DP),
            P(DP),
        ),
        check_vma=False,
    )
```

```python
import jax
import jax.numpy as jnp
from jax import lax
from jax.experimental import pallas as pl
from jax.experimental.pallas import tpu as pltpu
from jax.experimental.layout import Layout, with_layout_constraint
from jax.sharding import Mesh
from jax.sharding import PartitionSpec as P

HEAD = 64
OWN = 128
MASKED = -1e30
LAST = (((1,), (1,)), ((), ()))


def block_at(info, place):
    step = lax.rem(info[3] * (place // 2 - info[0]) + 4, 4)
    side = lax.rem(place % 2 + info[1], 2)
    index = jnp.where(step == 1, 2, jnp.where(step == 2, 1, step))
    index = jnp.where(side == 0, index, jnp.where(index == 0, 7, 3 + index))
    return pl.multiple_of(index * OWN, OWN)


def in_order(info, src, dst):
    for place in range(8):
        dst[place * OWN : (place + 1) * OWN, :] = src[pl.ds(block_at(info, place), OWN), :]


def head_of(values, head):
    lane = lax.broadcasted_iota(jnp.int32, values.shape, 1)
    return jnp.where(lane // HEAD == head, values, jnp.zeros_like(values))


def masked_scores(info, key_part, query_head, start):
    scores = lax.dot_general(key_part, query_head, LAST, preferred_element_type=jnp.float32)
    key_at = lax.broadcasted_iota(jnp.int32, scores.shape, 0)
    query_at = start + lax.broadcasted_iota(jnp.int32, (1, scores.shape[1]), 1)
    return jnp.where(key_at <= jnp.minimum(query_at, info[2] - 1), scores, MASKED)


def forward_kernel(info, qkv_ref, ctx_ref, lse_ref, qkv, v_flip):
    in_order(info, qkv_ref, qkv)
    v_flip[...] = qkv[:, 256:384].T
    step = 2 * OWN
    for i in range(4):
        n = (i + 1) * step
        queries = qkv[i * step : n, 0:128]
        parts = []
        for head in range(2):
            scores = masked_scores(info, qkv[0:n, 128:256], head_of(queries, head), i * step)
            top = jnp.max(scores, 0, keepdims=True)
            weights = jnp.exp(scores - top)
            total = jnp.sum(weights, 0, keepdims=True)
            product = jnp.dot(
                v_flip[head * HEAD : (head + 1) * HEAD, 0:n],
                weights.astype(jnp.bfloat16),
                preferred_element_type=jnp.float32,
            )
            parts.append(product * (1.0 / total))
            lse_ref[0, head : head + 1, i * step : n] = top + jnp.log(total)
        block = jnp.concatenate(parts, 0).T.astype(jnp.bfloat16)
        for half in range(2):
            ctx_ref[pl.ds(block_at(info, 2 * i + half), OWN), :] = block[half * OWN : (half + 1) * OWN]


def backward_kernel(info, qkv_ref, up_ref, lse_ref, out_ref, qkv, up, k_flip, dk, dv):
    in_order(info, qkv_ref, qkv)
    in_order(info, up_ref, up)
    k_flip[...] = qkv[:, 128:256].T
    step = 2 * OWN
    for i in (3, 2, 1, 0):
        n = (i + 1) * step
        queries = qkv[i * step : n, 0:128]
        upstream = up[i * step : n, :]
        parts = []
        for head in range(2):
            query_head = head_of(queries, head)
            up_head = head_of(upstream, head)
            scores = masked_scores(info, qkv[0:n, 128:256], query_head, i * step)
            soft = jnp.exp(scores - lse_ref[0, head : head + 1, i * step : n])
            value_part = jnp.dot(soft.astype(jnp.bfloat16), up_head, preferred_element_type=jnp.float32)
            grad_soft = lax.dot_general(qkv[0:n, 256:384], up_head, LAST, preferred_element_type=jnp.float32)
            weighted = jnp.sum(soft * grad_soft, 0, keepdims=True)
            grad_scores = (soft * (grad_soft - weighted)).astype(jnp.bfloat16)
            key_part = jnp.dot(grad_scores, query_head, preferred_element_type=jnp.float32)
            if i == 3 and head == 0:
                dv[...] = value_part
                dk[...] = key_part
            else:
                dv[0:n, :] += value_part
                dk[0:n, :] += key_part
            parts.append(
                jnp.dot(k_flip[head * HEAD : (head + 1) * HEAD, 0:n], grad_scores, preferred_element_type=jnp.float32)
            )
        block = jnp.concatenate(parts, 0).T.astype(jnp.bfloat16) * jnp.bfloat16(HEAD**-0.5)
        for half in range(2):
            out_ref[pl.ds(block_at(info, 2 * i + half), OWN), 0:128] = block[half * OWN : (half + 1) * OWN]
    for place in range(8):
        at = pl.ds(block_at(info, place), OWN)
        out_ref[at, 128:256] = dk[place * OWN : (place + 1) * OWN, :].astype(jnp.bfloat16)
        out_ref[at, 256:384] = dv[place * OWN : (place + 1) * OWN, :].astype(jnp.bfloat16)


def attend_forward(info, qkv):
    rows = qkv.shape[0]
    return pl.pallas_call(
        forward_kernel,
        grid=(2,),
        in_specs=[pl.BlockSpec(memory_space=pltpu.SMEM), pl.BlockSpec((rows, 384), lambda g: (0, g))],
        out_specs=[pl.BlockSpec((rows, 128), lambda g: (0, g)), pl.BlockSpec((1, 8, rows), lambda g: (g, 0, 0))],
        out_shape=[
            jax.ShapeDtypeStruct((rows, 256), jnp.bfloat16),
            jax.ShapeDtypeStruct((2, 8, rows), jnp.float32),
        ],
        scratch_shapes=[pltpu.VMEM((rows, 384), jnp.bfloat16), pltpu.VMEM((128, rows), jnp.bfloat16)],
        compiler_params=pltpu.CompilerParams(vmem_limit_bytes=20 * 1024 * 1024),
        cost_estimate=pl.CostEstimate(
            flops=16 * rows * rows * HEAD, bytes_accessed=4 * 1024 * 1024, transcendentals=2 * rows * rows
        ),
        name="attend_forward",
    )(info, qkv)


def attend_backward(info, qkv, upstream, lse, pair):
    rows = qkv.shape[0]
    return pl.pallas_call(
        backward_kernel,
        grid=(1,),
        in_specs=[
            pl.BlockSpec(memory_space=pltpu.SMEM),
            pl.BlockSpec((rows, 384), lambda g: (0, pair)),
            pl.BlockSpec((rows, 128), lambda g: (0, pair)),
            pl.BlockSpec((1, 8, rows), lambda g: (pair, 0, 0)),
        ],
        out_specs=pl.BlockSpec((rows, 384), lambda g: (0, 0)),
        out_shape=jax.ShapeDtypeStruct((rows, 384), jnp.bfloat16),
        scratch_shapes=[
            pltpu.VMEM((rows, 384), jnp.bfloat16),
            pltpu.VMEM((rows, 128), jnp.bfloat16),
            pltpu.VMEM((128, rows), jnp.bfloat16),
            pltpu.VMEM((rows, 128), jnp.float32),
            pltpu.VMEM((rows, 128), jnp.float32),
        ],
        compiler_params=pltpu.CompilerParams(vmem_limit_bytes=20 * 1024 * 1024),
        cost_estimate=pl.CostEstimate(
            flops=20 * rows * rows * HEAD, bytes_accessed=3 * 1024 * 1024, transcendentals=rows * rows
        ),
        name="attend_backward",
    )(info, qkv, upstream, lse)


LAYER = 12
EPS = 1e-05
TP = ("y", "zl", "core")
DP = ("x", "zh")
EVERY = ("y", "zl", "core", "x", "zh")
SIDE = ("zl", "core", "zh")
AHEAD = [(i * 2 + c, ((i + 1 - 2 * c) % 4) * 2 + c) for i in range(4) for c in range(2)]
BEHIND = [(b, a) for a, b in AHEAD]
AHEAD_X = [(c * 4 + i, c * 4 + (i + 1 - 2 * c) % 4) for i in range(4) for c in range(2)]
BEHIND_X = [(b, a) for a, b in AHEAD_X]


def spot(z, core):
    return ((z % 2) * 2 + core) * 2 + z // 2


def away(z, core):
    return z if core == 0 else (4 - z) % 4


PARTNER = [(spot(z, c), spot(z ^ 1 if c == 0 else 3 - z, c)) for z in range(4) for c in range(2)]
CROSS = [(spot(z, 0), spot(away(z, 1), 1)) for z in range(4)] + [(spot(z, 1), spot(z, 0)) for z in range(4)]
BACK = [(b, a) for a, b in CROSS]
MOVE = [(spot(z, c), spot(away(z, c), c)) for z in range(4) for c in range(2)]


def f32(values):
    return values.astype(jnp.float32)


def bf16(values):
    return values.astype(jnp.bfloat16)


def after(values, *earlier):
    earlier = [e for e in earlier if e is not None]
    return lax.optimization_barrier((values, earlier))[0] if earlier else values


def from_behind(values, axis="y"):
    return lax.ppermute(values, (axis, "core") if axis == "y" else ("core", axis), AHEAD if axis == "y" else AHEAD_X)


def from_ahead(values, axis="y"):
    return lax.ppermute(values, (axis, "core") if axis == "y" else ("core", axis), BEHIND if axis == "y" else BEHIND_X)


def from_side(values):
    return lax.ppermute(values, SIDE, PARTNER)


def from_core(values):
    return lax.ppermute(values, "core", [(0, 1), (1, 0)])


class Gather:
    def __init__(self, own):
        self.own = own
        self.behind, self.ahead, self.side = from_behind(own), from_ahead(own), from_side(own)

    def second(self, *earlier):
        behind, ahead = after((self.behind, self.ahead), self.side, *earlier)
        self.far = from_behind(behind)
        self.ahead_side, self.behind_side = from_side(ahead), from_side(behind)
        self.near = behind
        return self

    def third(self, *earlier):
        self.far_side = from_side(after(self.far, self.ahead_side, self.behind_side, *earlier))
        return self

    def first_half(self, *earlier):
        return jnp.concatenate(after((self.own, self.far, self.ahead, self.behind), *earlier), 0)

    def second_half(self, *earlier):
        far_side = after(self.far_side, *earlier)
        return jnp.concatenate((far_side, self.ahead_side, self.behind_side, self.side), 0)


class ProductSum:
    def __init__(self, left, right, dims=((1,), (0,))):
        rest, sides = left
        self.count = rest.shape[0] // 4

        def times(block, earlier=None):
            block = after(block, earlier)
            return bf16(lax.dot_general(block, right, (dims, ((), ())), preferred_element_type=jnp.float32))

        count = self.count
        self.times, self.last = times, sides[3 * count :]
        self.first = times(sides[:count])
        self.near_part, self.rest = times(sides[count : 3 * count]), times(rest)

    def kept(self, index):
        return f32(self.rest[index * self.count : (index + 1) * self.count])

    def start(self, *earlier):
        self.far_side = from_side(after(self.first, *earlier))
        return self

    def second(self, *earlier):
        far_side = after(self.far_side, *earlier)
        self.side_part = self.times(self.last, far_side)
        self.near_side = from_side(after(self.near_part, far_side))
        self.far = from_behind(bf16(self.kept(1) + f32(far_side)))
        return self

    def third(self, *earlier):
        near_side, far = after((self.near_side, self.far), *earlier)
        count = self.count
        self.sent = (
            bf16(self.kept(3) + f32(near_side[count:])),
            bf16(self.kept(2) + f32(near_side[:count]) + f32(far)),
        )
        self.behind, self.ahead = from_ahead(self.sent[0]), from_behind(self.sent[1])
        self.own_side = from_side(after(self.side_part, near_side))
        return self

    def total(self, *earlier):
        own_side, behind, ahead = after((self.own_side, self.behind, self.ahead), *earlier)
        return self.kept(0) + f32(own_side) + f32(behind) + f32(ahead)


def halved(values):
    half = values.shape[0] // 2
    return values[:half], values[half:]


class DpSum:
    def __init__(self, arrays, sign):
        self.place, self.zh = lax.axis_index("x"), lax.axis_index("zh")
        count = arrays[0].shape[0] // 4

        def block(step):
            at = lax.rem(self.place + sign * step + 4, 4) * count
            return jnp.concatenate([lax.dynamic_slice_in_dim(a, at, count, 0) for a in arrays], 1)

        self.sent = (block(2), block(-1))
        self.far = from_behind(self.sent[0], "x")
        self.behind = from_ahead(self.sent[1], "x")
        self.to_ahead, self.own = block(1), block(0)

    def second(self, *earlier):
        far = after(self.far, *earlier)
        self.to_ahead = bf16(f32(self.to_ahead) + f32(far))
        self.ahead = from_behind(self.to_ahead, "x")
        return self

    def third(self, *earlier):
        behind, ahead = after((self.behind, self.ahead), *earlier)
        total = f32(self.own) + f32(behind) + f32(ahead)
        half = total.shape[0] // 2
        self.mine = lax.dynamic_slice_in_dim(total, self.zh * half, half, 0)
        other = lax.dynamic_slice_in_dim(total, (1 - self.zh) * half, half, 0)
        self.other = lax.ppermute(bf16(other), "zh", [(0, 1), (1, 0)])
        return self

    def total(self, *earlier):
        return self.mine + f32(after(self.other, *earlier))


def norm_rows(values, gain, shift):
    average = jnp.mean(values, -1, keepdims=True)
    centred = values - average
    variance = jnp.mean(centred * centred, -1, keepdims=True)
    inverse = lax.rsqrt(variance + EPS)
    normed = centred * inverse
    return normed, inverse, normed * gain + shift


def norm_back(upstream, normed, inverse, gain):
    scaled = upstream * gain
    mean_term = jnp.mean(scaled, -1, keepdims=True)
    proj_term = jnp.mean(scaled * normed, -1, keepdims=True)
    return inverse * (scaled - mean_term - normed * proj_term)


def across(left, right):
    return lax.dot_general(left, right, (((0,), (0,)), ((), ())), preferred_element_type=jnp.float32)


def times_columns(weights, columns):
    high = bf16(columns)
    pair = jnp.concatenate([high, bf16(columns - f32(high))], 0)
    product = lax.dot_general(pair, weights, (((1,), (1,)), ((), ())), preferred_element_type=jnp.float32)
    return jnp.sum(product, 0, keepdims=True)


def column_sums(values):
    return jnp.sum(f32(values), 0, keepdims=True)


class GradSum:
    def __init__(self, left, other):
        self.left = left
        self.sent = bf16(across(left, other))
        self.received = from_core(self.sent)

    def total(self, own, *earlier):
        left, own, received = after((self.left, own, self.received), *earlier)
        return bf16(across(left, own) + f32(received))


def on_device(
    tokens,
    lengths,
    exit_layers,
    weight_query,
    bias_query,
    weight_key,
    weight_value,
    bias_value,
    weight_out,
    bias_out,
    weight_up,
    bias_up,
    weight_down,
    bias_down,
    gain_in,
    shift_in,
    gain_mid,
    shift_mid,
    cotangent,
):
    row, side, core = lax.axis_index("y"), lax.axis_index("zl"), lax.axis_index("core")
    dp_index = lax.axis_index("x") * 2 + lax.axis_index("zh")
    tp_index = (row * 2 + side) * 2 + core
    first_core = core == 0
    features = tokens.shape[-1]
    seq_len = exit_layers.shape[1]
    head_cols = weight_query.shape[1]
    hidden = weight_up.shape[1]
    own_rows = 2 * tokens.shape[1]

    def to_own(values):
        crossed = lax.ppermute(jnp.where(first_core, values[1], values[0]), SIDE, CROSS)
        moved = lax.ppermute(values[1], SIDE, MOVE)
        return crossed, moved

    def owned(values, crossed, moved):
        return jnp.concatenate(
            [jnp.where(first_core, values[0], crossed), jnp.where(first_core, crossed, moved)], 0
        )

    def to_home(values):
        first, second = values[: own_rows // 2], values[own_rows // 2 :]
        crossed = lax.ppermute(jnp.where(first_core, second, first), SIDE, BACK)
        moved = lax.ppermute(second, SIDE, MOVE)
        crossed = (f32(crossed) + 0.0 * f32(moved[:1, :1])).astype(crossed.dtype)
        return jnp.stack([jnp.where(first_core, first, crossed), jnp.where(first_core, crossed, moved)], 0)

    width = 3 * head_cols
    part = features // 8
    with jax.named_scope("own_rows"):
        tokens_own = f32(owned(tokens, *to_own(tokens)))
        normed_in, inverse_in, normed_out = norm_rows(tokens_own, gain_in, shift_in)
        normed_out = bf16(normed_out)
    with jax.named_scope("gather_in"):
        gathered_in = Gather(normed_out)
    with jax.named_scope("chip_weights"):
        biases = jnp.concatenate([bias_query, bias_value, bias_up])
        cotangent, exit_layers, lengths = after((cotangent, exit_layers, lengths), normed_out)
        weight_query, weight_key, weight_value = after((weight_query, weight_key, weight_value), gathered_in.side)
        joined = jnp.concatenate([weight_query, weight_key, weight_value], 1)
    with jax.named_scope("cotangent_rows"):
        cotangent_parts = to_own(cotangent)
        about = jnp.concatenate([exit_layers[1], jnp.broadcast_to(lengths[1:], (128,))], 0)
        moved_about = lax.ppermute(about, SIDE, MOVE)
    with jax.named_scope("gather_in"):
        gathered_in.second(joined)
    with jax.named_scope("chip_weights"):
        joined, weight_out, biases, weight_up, weight_down = after(
            (joined, weight_out, biases, weight_up, weight_down), gathered_in.near
        )
        joined_core = from_core(joined)
        weight_out_core, biases_core = from_core(weight_out), from_core(biases)
        weight_up_core, weight_down_core = from_core(weight_up), from_core(weight_down)
        weight_qkv = with_layout_constraint(
            jnp.concatenate(after([joined, joined_core], gathered_in.far), 1), Layout((0, 1))
        )

    with jax.named_scope("cotangent_rows"):
        cotangent_parts, moved_about = after((cotangent_parts, moved_about), gathered_in.far)
        cotangent_own = f32(owned(cotangent, *cotangent_parts))
        positions = jnp.arange(seq_len)
        exits = jnp.where(first_core, exit_layers[0], moved_about[:seq_len])
        length = jnp.where(first_core, lengths[0], moved_about[seq_len])
        live_all = f32((positions < length) & (exits >= LAYER))
        live_own = lax.dynamic_slice_in_dim(live_all, (row * 2 + side) * own_rows, own_rows, 0)[:, None]
        sign = 1 - 2 * core
        info = jnp.stack([row, side, length, sign]).astype(jnp.int32)
        grad_own = cotangent_own * live_own
        grad_own_low = bf16(grad_own)
    with jax.named_scope("gather_in"):
        gathered_in.third()
    with jax.named_scope("project"):
        first_in = gathered_in.first_half(weight_qkv, grad_own_low)
        scale = HEAD**-0.5
        none = jnp.zeros((head_cols,), jnp.float32)
        bias_qkv = jnp.concatenate(
            [biases[:head_cols], none, biases[head_cols : 2 * head_cols]]
            + [biases_core[:head_cols], none, biases_core[head_cols : 2 * head_cols]]
        )
        scale_qkv = jnp.tile(jnp.concatenate([none + scale, none + 1.0, none + 1.0]), 2)
        bias_up_chip = jnp.concatenate([biases[2 * head_cols :], biases_core[2 * head_cols :]])

        def projected(rows):
            product = jnp.dot(rows, weight_qkv, preferred_element_type=jnp.float32)
            return bf16((product + bias_qkv) * scale_qkv)

        first_qkv = projected(first_in)
        second_in = gathered_in.second_half(first_qkv)
        qkv = jnp.concatenate([first_qkv, projected(second_in)], 0)
        hidden_in = jnp.concatenate(after([first_in, second_in], qkv), 0)
    with jax.named_scope("chip_weights"):
        weight_out_chip = jnp.concatenate([weight_out, weight_out_core], 0)
        weight_out_chip, weight_up_core, weight_down_core = after(
            (weight_out_chip, weight_up_core, weight_down_core), gathered_in.far
        )
    with jax.named_scope("gather_cotangent"):
        gathered_grad = Gather(after(grad_own_low, qkv))
    context, lse = attend_forward(info, after(qkv, weight_out_chip, weight_up_core, weight_down_core))
    with jax.named_scope("sum_attention"):
        sum_att = ProductSum(halved(context), weight_out_chip).start().second()
    with jax.named_scope("chip_weights"):
        up_own, up_core, down_own, down_core = after(
            (weight_up, weight_up_core, weight_down, weight_down_core), sum_att.far_side
        )
        weight_up_chip = jnp.concatenate([up_own, up_core], 1)
        weight_down_chip = jnp.concatenate([down_own, down_core], 0)
    with jax.named_scope("sum_attention"):
        sum_att.third(weight_up_chip, weight_down_chip)
    with jax.named_scope("gather_cotangent"):
        gathered_grad.second(sum_att.far, sum_att.near_side)
    with jax.named_scope("sum_attention"):
        attention = sum_att.total()
    with jax.named_scope("gather_mid"):
        mid_own = tokens_own + live_own * (attention + bias_out)
        normed_mid, inverse_mid, mid_out = norm_rows(mid_own, gain_mid, shift_mid)
        mid_out = bf16(mid_out)
        gathered_mid = Gather(mid_out)
    with jax.named_scope("gather_cotangent"):
        gathered_grad.third(mid_out)
    with jax.named_scope("gather_mid"):
        gathered_mid.second()
    with jax.named_scope("feed_forward"):
        live_halves = (gathered_grad.first_half(gathered_mid.near), gathered_grad.second_half(gathered_mid.near))
        grad_activated = lax.optimization_barrier(
            [
                lax.dot_general(
                    half, weight_down_chip, (((1,), (1,)), ((), ())), preferred_element_type=jnp.float32
                )
                for half in live_halves
            ]
        )
    def fed(rows, upstream):
        up_sum = jnp.dot(rows, weight_up_chip, preferred_element_type=jnp.float32) + bias_up_chip
        return bf16(jax.nn.gelu(up_sum)), bf16(jax.vjp(jax.nn.gelu, up_sum)[1](upstream)[0])

    with jax.named_scope("feed_forward"):
        first_mid = gathered_mid.third().first_half(*grad_activated)
        first_fed = fed(first_mid, grad_activated[0])
        second_mid = gathered_mid.second_half(*first_fed)
        mid_halves = (first_mid, second_mid)
        activated, grad_up_sum = zip(first_fed, fed(second_mid, grad_activated[1]))
    with jax.named_scope("sum_mid_grad"):
        sum_mid = ProductSum(grad_up_sum, weight_up_chip, ((1,), (1,))).start().second()
    with jax.named_scope("feed_forward"):
        hidden_mid, grad_live, all_activated, all_grad_up = after(
            [jnp.concatenate(pair, 0) for pair in (mid_halves, live_halves, activated, grad_up_sum)], sum_mid.far_side
        )
    with jax.named_scope("sum_branch"):
        sum_branch = ProductSum(after(activated, sum_mid.far_side), weight_down_chip)
    with jax.named_scope("grads_mlp"):
        early_up, early_act = after((all_grad_up, all_activated), sum_mid.far, sum_mid.near_side)
        grads_up = GradSum(hidden_mid, early_up[:, hidden:])
        grads_down = GradSum(grad_live, early_act[:, hidden:])
    with jax.named_scope("sum_mid_grad"):
        sum_mid.third(sum_branch.first, sum_branch.near_part, sum_branch.rest)
        mid_grad = sum_mid.total(grads_up.sent, grads_down.sent)
    with jax.named_scope("sum_branch"):
        sum_branch.start(*sum_mid.sent)
    with jax.named_scope("gather_back"):
        back_own = cotangent_own + norm_back(mid_grad, normed_mid, inverse_mid, gain_mid)
        back_live = back_own * live_own
        back_low_own = bf16(back_live)
        gathered_back = Gather(back_low_own)
    with jax.named_scope("grads_mlp"):
        grad_up = grads_up.total(all_grad_up[:, :hidden], back_low_own)
        grad_down = grads_down.total(all_activated[:, :hidden], back_low_own)
    with jax.named_scope("gather_back"):
        gathered_back.second(grad_up, grad_down)
    with jax.named_scope("dp_mlp"):
        dp_mlp = DpSum(after([grad_up, grad_down], gathered_back.near), sign)
    with jax.named_scope("sum_branch"):
        sum_branch.second(gathered_back.near)
    with jax.named_scope("early_lines"):
        early_up = after(all_grad_up, gathered_back.far)
        early_vectors = after(
            [
                column_sums(mid_grad * normed_mid),
                column_sums(mid_grad),
                column_sums(back_live),
                column_sums(grad_own),
            ],
            gathered_back.far,
        )
        column_up = column_sums(early_up)
    with jax.named_scope("gather_back"):
        gathered_back.third(*dp_mlp.sent)
    with jax.named_scope("gather_back"):
        first_back = gathered_back.first_half()

    with jax.named_scope("grad_context"):

        def to_context(rows):
            product = lax.dot_general(
                rows, weight_out_chip, (((1,), (1,)), ((), ())), preferred_element_type=jnp.float32
            )
            return bf16(product)

        context_halves = halved(context)
        first_context = to_context(first_back)
        first_product = across(first_back, context_halves[0])
        second_back = gathered_back.second_half(first_context, first_product)
        grad_context = jnp.concatenate([first_context, to_context(second_back)], 0)
    with jax.named_scope("grads_attention"):
        product_out = first_product + across(after(second_back, grad_context), context_halves[1])
        product_own, product_core = product_out[:, :head_cols], bf16(product_out[:, head_cols:])
        received_out = from_core(product_core)
    grad_qkv_core = attend_backward(info, qkv, after(grad_context, product_own, product_core), lse, 1)
    with jax.named_scope("dp_mlp"):
        dp_mlp.second(grad_qkv_core)
    with jax.named_scope("sum_branch"):
        sum_branch.third(grad_context)
    with jax.named_scope("grads_attention"):
        grads_in = GradSum(hidden_in, grad_qkv_core)
        grad_out = bf16(product_own + f32(after(received_out, grad_qkv_core)))
        columns_core = column_sums(grad_qkv_core)
        shift_core = times_columns(weight_qkv[:, width:], columns_core)
    grad_qkv_own = attend_backward(
        info,
        qkv,
        after(grad_context, grads_in.received, grad_out, shift_core, column_up, early_vectors, dp_mlp.to_ahead, sum_branch.sent),
        lse,
        0,
    )
    with jax.named_scope("sum_in_grad"):
        grad_qkv = jnp.concatenate([grad_qkv_own, grad_qkv_core], 1)
        sum_in = ProductSum(halved(grad_qkv), weight_qkv, ((1,), (1,))).start()
    with jax.named_scope("sum_in_grad"):
        sum_in.second()
    with jax.named_scope("grads_attention"):
        grad_in = grads_in.total(grad_qkv_own, sum_in.side_part)
    with jax.named_scope("dp_attention"):
        dp_attention = DpSum([grad_in, grad_out], sign)
    with jax.named_scope("dp_mlp"):
        dp_mlp.third(sum_in.side_part)
    with jax.named_scope("sum_in_grad"):
        sum_in.third(*dp_attention.sent)
    with jax.named_scope("dp_attention"):
        dp_attention.second(*sum_in.sent)

    def of_dp(values):
        return lax.dynamic_slice_in_dim(values, dp_index * part, part, 0)

    with jax.named_scope("small_sums"):
        columns_own = column_sums(after(grad_qkv_own, *sum_in.sent))
        shift_in_part = shift_core + times_columns(weight_qkv[:, :width], columns_own)
        gain_in_part = jnp.sum(f32(after(grad_in, *sum_in.sent)) * f32(weight_qkv[:, :width]), 1)
        vectors = [v.reshape(8, part) for v in (shift_in_part, *early_vectors, gain_in_part)]
        sums = [column_up[:, :hidden], columns_own[:, :head_cols], columns_own[:, 2 * head_cols :]]
        sums += [column_up[:, hidden:], columns_core[:, :head_cols], columns_core[:, 2 * head_cols :]]
        lines = jnp.concatenate(vectors + [v.reshape(8, -1) for v in sums], 1)
        lines = after(jnp.pad(lines, ((0, 0), (0, -lines.shape[1] % 128))), dp_attention.to_ahead)
        small = jnp.sum(lax.all_to_all(lines, DP, 0, 0, tiled=True), 0)
    with jax.named_scope("sum_branch"):
        branch = sum_branch.total(*sum_in.sent)
        output_own = bf16(mid_own + live_own * (branch + bias_down))
    with jax.named_scope("sum_in_grad"):
        in_grad = sum_in.total(dp_attention.to_ahead, output_own)
    with jax.named_scope("dp_attention"):
        dp_attention.third(in_grad)
    with jax.named_scope("tokens_grad"):
        tokens_grad_own = bf16(back_own + norm_back(in_grad, normed_in, inverse_in, gain_in))
        grad_tokens = f32(to_home(tokens_grad_own))
    with jax.named_scope("sum_branch"):
        output = to_home(after(output_own, tokens_grad_own))
    with jax.named_scope("small_sums"):
        to_all = small[: 6 * part]
        wide, narrow = hidden // 8, head_cols // 8
        at = 6 * part + wide + 2 * narrow
        own_biases, side_biases = small[6 * part : at], small[at : at + wide + 2 * narrow]
        dest = jnp.arange(16)[:, None]
        for_biases = jnp.where(dest == tp_index, own_biases, jnp.where(dest == (tp_index ^ 1), side_biases, 0.0))
        sent = jnp.concatenate([jnp.broadcast_to(to_all, (16, 6 * part)), for_biases], 1)
        sent = after(jnp.pad(sent, ((0, 0), (0, -sent.shape[1] % 128))), tokens_grad_own)
        small = jnp.sum(lax.all_to_all(sent, TP, 0, 0, tiled=True), 0)
        vectors = small[: 6 * part].reshape(6, part)
        up_part, query_part, value_part = (
            small[6 * part + a : 6 * part + b]
            for a, b in ((0, wide), (wide, wide + narrow), (wide + narrow, wide + 2 * narrow))
        )

    with jax.named_scope("dp_attention"):
        summed_attention = dp_attention.total(tokens_grad_own)
    with jax.named_scope("dp_mlp"):
        summed_mlp = dp_mlp.total(tokens_grad_own)

    return (
        output,
        grad_tokens,
        summed_attention[:, :head_cols],
        query_part,
        summed_attention[:, head_cols : 2 * head_cols],
        summed_attention[:, 2 * head_cols : width],
        value_part,
        summed_attention[:, width : width + head_cols].T,
        vectors[3],
        summed_mlp[:, :hidden],
        up_part,
        summed_mlp[:, hidden:].T,
        vectors[4],
        (vectors[5] - of_dp(shift_in) * vectors[0]) / of_dp(gain_in),
        vectors[0],
        vectors[1],
        vectors[2],
    )


def solution(mesh):
    names = Mesh(mesh.devices.reshape(4, 2, 2, 4, 2), EVERY)
    residual = P(DP, TP, None)
    return jax.shard_map(
        on_device,
        mesh=names,
        in_specs=(
            residual,
            P(DP),
            P(DP, None),
            P(None, TP),
            P(TP),
            P(None, TP),
            P(None, TP),
            P(TP),
            P(TP, None),
            P(),
            P(None, TP),
            P(TP),
            P(TP, None),
            P(),
            P(),
            P(),
            P(),
            P(),
            residual,
        ),
        out_specs=(
            residual,
            residual,
            P(DP, TP),
            P(EVERY),
            P(DP, TP),
            P(DP, TP),
            P(EVERY),
            P(TP, DP),
            P(DP),
            P(DP, TP),
            P(EVERY),
            P(TP, DP),
            P(DP),
            P(DP),
            P(DP),
            P(DP),
            P(DP),
        ),
        check_vma=False,
    )
```

```python
import jax
import jax.numpy as jnp
from jax import lax
from jax.experimental import pallas as pl
from jax.experimental.pallas import tpu as pltpu
from jax.experimental.layout import Layout, with_layout_constraint
from jax.sharding import Mesh
from jax.sharding import PartitionSpec as P

HEAD = 64
OWN = 128
MASKED = -1e30
LAST = (((1,), (1,)), ((), ()))


def block_at(info, place):
    step = lax.rem(info[3] * (place // 2 - info[0]) + 4, 4)
    side = lax.rem(place % 2 + info[1], 2)
    index = jnp.where(step == 1, 2, jnp.where(step == 2, 1, step))
    index = jnp.where(side == 0, index, jnp.where(index == 0, 7, 3 + index))
    return pl.multiple_of(index * OWN, OWN)


def in_order(info, src, dst):
    for place in range(8):
        dst[place * OWN : (place + 1) * OWN, :] = src[pl.ds(block_at(info, place), OWN), :]


def head_of(values, head):
    lane = lax.broadcasted_iota(jnp.int32, values.shape, 1)
    return jnp.where(lane // HEAD == head, values, jnp.zeros_like(values))


def masked_scores(info, key_part, query_head, start):
    scores = lax.dot_general(key_part, query_head, LAST, preferred_element_type=jnp.float32)
    key_at = lax.broadcasted_iota(jnp.int32, scores.shape, 0)
    query_at = start + lax.broadcasted_iota(jnp.int32, (1, scores.shape[1]), 1)
    return jnp.where(key_at <= jnp.minimum(query_at, info[2] - 1), scores, MASKED)


def forward_kernel(info, qkv_ref, ctx_ref, lse_ref, qkv, v_flip):
    in_order(info, qkv_ref, qkv)
    v_flip[...] = qkv[:, 256:384].T
    step = 2 * OWN
    for i in range(4):
        n = (i + 1) * step
        queries = qkv[i * step : n, 0:128]
        parts = []
        for head in range(2):
            scores = masked_scores(info, qkv[0:n, 128:256], head_of(queries, head), i * step)
            top = jnp.max(scores, 0, keepdims=True)
            weights = jnp.exp(scores - top)
            total = jnp.sum(weights, 0, keepdims=True)
            soft = (weights * (1.0 / total)).astype(jnp.bfloat16)
            parts.append(
                jnp.dot(v_flip[head * HEAD : (head + 1) * HEAD, 0:n], soft, preferred_element_type=jnp.float32)
            )
            lse_ref[0, head : head + 1, i * step : n] = top + jnp.log(total)
        block = jnp.concatenate(parts, 0).T.astype(jnp.bfloat16)
        for half in range(2):
            ctx_ref[pl.ds(block_at(info, 2 * i + half), OWN), :] = block[half * OWN : (half + 1) * OWN]


def backward_kernel(info, qkv_ref, up_ref, lse_ref, out_ref, qkv, up, k_flip, dk, dv):
    in_order(info, qkv_ref, qkv)
    in_order(info, up_ref, up)
    k_flip[...] = qkv[:, 128:256].T
    step = 2 * OWN
    for i in (3, 2, 1, 0):
        n = (i + 1) * step
        queries = qkv[i * step : n, 0:128]
        upstream = up[i * step : n, :]
        parts = []
        for head in range(2):
            query_head = head_of(queries, head)
            up_head = head_of(upstream, head)
            scores = masked_scores(info, qkv[0:n, 128:256], query_head, i * step)
            soft = jnp.exp(scores - lse_ref[0, head : head + 1, i * step : n])
            value_part = jnp.dot(soft.astype(jnp.bfloat16), up_head, preferred_element_type=jnp.float32)
            grad_soft = lax.dot_general(qkv[0:n, 256:384], up_head, LAST, preferred_element_type=jnp.float32)
            weighted = jnp.sum(soft * grad_soft, 0, keepdims=True)
            grad_scores = (soft * (grad_soft - weighted)).astype(jnp.bfloat16)
            key_part = jnp.dot(grad_scores, query_head, preferred_element_type=jnp.float32)
            if i == 3 and head == 0:
                dv[...] = value_part
                dk[...] = key_part
            else:
                dv[0:n, :] += value_part
                dk[0:n, :] += key_part
            parts.append(
                jnp.dot(k_flip[head * HEAD : (head + 1) * HEAD, 0:n], grad_scores, preferred_element_type=jnp.float32)
            )
        block = jnp.concatenate(parts, 0).T.astype(jnp.bfloat16) * jnp.bfloat16(HEAD**-0.5)
        for half in range(2):
            out_ref[pl.ds(block_at(info, 2 * i + half), OWN), 0:128] = block[half * OWN : (half + 1) * OWN]
    for place in range(8):
        at = pl.ds(block_at(info, place), OWN)
        out_ref[at, 128:256] = dk[place * OWN : (place + 1) * OWN, :].astype(jnp.bfloat16)
        out_ref[at, 256:384] = dv[place * OWN : (place + 1) * OWN, :].astype(jnp.bfloat16)


def attend_forward(info, qkv):
    rows = qkv.shape[0]
    return pl.pallas_call(
        forward_kernel,
        grid=(2,),
        in_specs=[pl.BlockSpec(memory_space=pltpu.SMEM), pl.BlockSpec((rows, 384), lambda g: (0, g))],
        out_specs=[pl.BlockSpec((rows, 128), lambda g: (0, g)), pl.BlockSpec((1, 8, rows), lambda g: (g, 0, 0))],
        out_shape=[
            jax.ShapeDtypeStruct((rows, 256), jnp.bfloat16),
            jax.ShapeDtypeStruct((2, 8, rows), jnp.float32),
        ],
        scratch_shapes=[pltpu.VMEM((rows, 384), jnp.bfloat16), pltpu.VMEM((128, rows), jnp.bfloat16)],
        compiler_params=pltpu.CompilerParams(vmem_limit_bytes=20 * 1024 * 1024),
        cost_estimate=pl.CostEstimate(
            flops=16 * rows * rows * HEAD, bytes_accessed=4 * 1024 * 1024, transcendentals=2 * rows * rows
        ),
        name="attend_forward",
    )(info, qkv)


def attend_backward(info, qkv, upstream, lse, pair):
    rows = qkv.shape[0]
    return pl.pallas_call(
        backward_kernel,
        grid=(1,),
        in_specs=[
            pl.BlockSpec(memory_space=pltpu.SMEM),
            pl.BlockSpec((rows, 384), lambda g: (0, pair)),
            pl.BlockSpec((rows, 128), lambda g: (0, pair)),
            pl.BlockSpec((1, 8, rows), lambda g: (pair, 0, 0)),
        ],
        out_specs=pl.BlockSpec((rows, 384), lambda g: (0, 0)),
        out_shape=jax.ShapeDtypeStruct((rows, 384), jnp.bfloat16),
        scratch_shapes=[
            pltpu.VMEM((rows, 384), jnp.bfloat16),
            pltpu.VMEM((rows, 128), jnp.bfloat16),
            pltpu.VMEM((128, rows), jnp.bfloat16),
            pltpu.VMEM((rows, 128), jnp.float32),
            pltpu.VMEM((rows, 128), jnp.float32),
        ],
        compiler_params=pltpu.CompilerParams(vmem_limit_bytes=20 * 1024 * 1024),
        cost_estimate=pl.CostEstimate(
            flops=20 * rows * rows * HEAD, bytes_accessed=3 * 1024 * 1024, transcendentals=rows * rows
        ),
        name="attend_backward",
    )(info, qkv, upstream, lse)


LAYER = 12
EPS = 1e-05
TP = ("y", "zl", "core")
DP = ("x", "zh")
EVERY = ("y", "zl", "core", "x", "zh")
SIDE = ("zl", "core", "zh")
AHEAD = [(i * 2 + c, ((i + 1 - 2 * c) % 4) * 2 + c) for i in range(4) for c in range(2)]
BEHIND = [(b, a) for a, b in AHEAD]
AHEAD_X = [(c * 4 + i, c * 4 + (i + 1 - 2 * c) % 4) for i in range(4) for c in range(2)]
BEHIND_X = [(b, a) for a, b in AHEAD_X]


def spot(z, core):
    return ((z % 2) * 2 + core) * 2 + z // 2


def away(z, core):
    return z if core == 0 else (4 - z) % 4


PARTNER = [(spot(z, c), spot(z ^ 1 if c == 0 else 3 - z, c)) for z in range(4) for c in range(2)]
CROSS = [(spot(z, 0), spot(away(z, 1), 1)) for z in range(4)] + [(spot(z, 1), spot(z, 0)) for z in range(4)]
BACK = [(b, a) for a, b in CROSS]
MOVE = [(spot(z, c), spot(away(z, c), c)) for z in range(4) for c in range(2)]


def f32(values):
    return values.astype(jnp.float32)


def bf16(values):
    return values.astype(jnp.bfloat16)


def after(values, *earlier):
    earlier = [e for e in earlier if e is not None]
    return lax.optimization_barrier((values, earlier))[0] if earlier else values


def from_behind(values, axis="y"):
    return lax.ppermute(values, (axis, "core") if axis == "y" else ("core", axis), AHEAD if axis == "y" else AHEAD_X)


def from_ahead(values, axis="y"):
    return lax.ppermute(values, (axis, "core") if axis == "y" else ("core", axis), BEHIND if axis == "y" else BEHIND_X)


def from_side(values):
    return lax.ppermute(values, SIDE, PARTNER)


def from_core(values):
    return lax.ppermute(values, "core", [(0, 1), (1, 0)])


class Gather:
    def __init__(self, own):
        self.own = own
        self.behind, self.ahead, self.side = from_behind(own), from_ahead(own), from_side(own)

    def second(self, *earlier):
        behind, ahead = after((self.behind, self.ahead), self.side, *earlier)
        self.far = from_behind(behind)
        self.ahead_side, self.behind_side = from_side(ahead), from_side(behind)
        self.near = behind
        return self

    def third(self, *earlier):
        self.far_side = from_side(after(self.far, self.ahead_side, self.behind_side, *earlier))
        return self

    def first_half(self, *earlier):
        return jnp.concatenate(after((self.own, self.far, self.ahead, self.behind), *earlier), 0)

    def second_half(self, *earlier):
        far_side = after(self.far_side, *earlier)
        return jnp.concatenate((far_side, self.ahead_side, self.behind_side, self.side), 0)


class ProductSum:
    def __init__(self, left, right, dims=((1,), (0,))):
        rest, sides = left
        self.count = rest.shape[0] // 4

        def times(block, earlier=None):
            block = after(block, earlier)
            return bf16(lax.dot_general(block, right, (dims, ((), ())), preferred_element_type=jnp.float32))

        count = self.count
        self.times, self.last = times, sides[3 * count :]
        self.first = times(sides[:count])
        self.near_part, self.rest = times(sides[count : 3 * count]), times(rest)

    def kept(self, index):
        return f32(self.rest[index * self.count : (index + 1) * self.count])

    def start(self, *earlier):
        self.far_side = from_side(after(self.first, *earlier))
        return self

    def second(self, *earlier):
        far_side = after(self.far_side, *earlier)
        self.side_part = self.times(self.last, far_side)
        self.near_side = from_side(after(self.near_part, far_side))
        self.far = from_behind(bf16(self.kept(1) + f32(far_side)))
        return self

    def third(self, *earlier):
        near_side, far = after((self.near_side, self.far), *earlier)
        count = self.count
        self.sent = (
            bf16(self.kept(3) + f32(near_side[count:])),
            bf16(self.kept(2) + f32(near_side[:count]) + f32(far)),
        )
        self.behind, self.ahead = from_ahead(self.sent[0]), from_behind(self.sent[1])
        self.own_side = from_side(after(self.side_part, near_side))
        return self

    def total(self, *earlier):
        own_side, behind, ahead = after((self.own_side, self.behind, self.ahead), *earlier)
        return self.kept(0) + f32(own_side) + f32(behind) + f32(ahead)


def halved(values):
    half = values.shape[0] // 2
    return values[:half], values[half:]


class DpSum:
    def __init__(self, arrays, sign):
        self.place, self.zh = lax.axis_index("x"), lax.axis_index("zh")
        count = arrays[0].shape[0] // 4

        def block(step):
            at = lax.rem(self.place + sign * step + 4, 4) * count
            return jnp.concatenate([lax.dynamic_slice_in_dim(a, at, count, 0) for a in arrays], 1)

        self.sent = (block(2), block(-1))
        self.far = from_behind(self.sent[0], "x")
        self.behind = from_ahead(self.sent[1], "x")
        self.to_ahead, self.own = block(1), block(0)

    def second(self, *earlier):
        far = after(self.far, *earlier)
        self.to_ahead = bf16(f32(self.to_ahead) + f32(far))
        self.ahead = from_behind(self.to_ahead, "x")
        return self

    def third(self, *earlier):
        behind, ahead = after((self.behind, self.ahead), *earlier)
        total = f32(self.own) + f32(behind) + f32(ahead)
        half = total.shape[0] // 2
        self.mine = lax.dynamic_slice_in_dim(total, self.zh * half, half, 0)
        other = lax.dynamic_slice_in_dim(total, (1 - self.zh) * half, half, 0)
        self.other = lax.ppermute(bf16(other), "zh", [(0, 1), (1, 0)])
        return self

    def total(self, *earlier):
        return self.mine + f32(after(self.other, *earlier))


def norm_rows(values, gain, shift):
    average = jnp.mean(values, -1, keepdims=True)
    centred = values - average
    variance = jnp.mean(centred * centred, -1, keepdims=True)
    inverse = lax.rsqrt(variance + EPS)
    normed = centred * inverse
    return normed, inverse, normed * gain + shift


def norm_back(upstream, normed, inverse, gain):
    scaled = upstream * gain
    mean_term = jnp.mean(scaled, -1, keepdims=True)
    proj_term = jnp.mean(scaled * normed, -1, keepdims=True)
    return inverse * (scaled - mean_term - normed * proj_term)


def across(left, right):
    return lax.dot_general(left, right, (((0,), (0,)), ((), ())), preferred_element_type=jnp.float32)


def times_columns(weights, columns):
    high = bf16(columns)
    pair = jnp.concatenate([high, bf16(columns - f32(high))], 0)
    product = lax.dot_general(pair, weights, (((1,), (1,)), ((), ())), preferred_element_type=jnp.float32)
    return jnp.sum(product, 0, keepdims=True)


def column_sums(values):
    return jnp.sum(f32(values), 0, keepdims=True)


class GradSum:
    def __init__(self, left, other):
        self.left = left
        self.sent = bf16(across(left, other))
        self.received = from_core(self.sent)

    def total(self, own, *earlier):
        left, own, received = after((self.left, own, self.received), *earlier)
        return bf16(across(left, own) + f32(received))


def on_device(
    tokens,
    lengths,
    exit_layers,
    weight_query,
    bias_query,
    weight_key,
    weight_value,
    bias_value,
    weight_out,
    bias_out,
    weight_up,
    bias_up,
    weight_down,
    bias_down,
    gain_in,
    shift_in,
    gain_mid,
    shift_mid,
    cotangent,
):
    row, side, core = lax.axis_index("y"), lax.axis_index("zl"), lax.axis_index("core")
    dp_index = lax.axis_index("x") * 2 + lax.axis_index("zh")
    tp_index = (row * 2 + side) * 2 + core
    first_core = core == 0
    features = tokens.shape[-1]
    seq_len = exit_layers.shape[1]
    head_cols = weight_query.shape[1]
    hidden = weight_up.shape[1]
    own_rows = 2 * tokens.shape[1]

    def to_own(values):
        crossed = lax.ppermute(jnp.where(first_core, values[1], values[0]), SIDE, CROSS)
        moved = lax.ppermute(values[1], SIDE, MOVE)
        return crossed, moved

    def owned(values, crossed, moved):
        return jnp.concatenate(
            [jnp.where(first_core, values[0], crossed), jnp.where(first_core, crossed, moved)], 0
        )

    def to_home(values):
        first, second = values[: own_rows // 2], values[own_rows // 2 :]
        crossed = lax.ppermute(jnp.where(first_core, second, first), SIDE, BACK)
        moved = lax.ppermute(second, SIDE, MOVE)
        crossed = (f32(crossed) + 0.0 * f32(moved[:1, :1])).astype(crossed.dtype)
        return jnp.stack([jnp.where(first_core, first, crossed), jnp.where(first_core, crossed, moved)], 0)

    width = 3 * head_cols
    part = features // 8
    with jax.named_scope("own_rows"):
        tokens_own = f32(owned(tokens, *to_own(tokens)))
        normed_in, inverse_in, normed_out = norm_rows(tokens_own, gain_in, shift_in)
        normed_out = bf16(normed_out)
    with jax.named_scope("gather_in"):
        gathered_in = Gather(normed_out)
    with jax.named_scope("chip_weights"):
        biases = jnp.concatenate([bias_query, bias_value, bias_up])
        cotangent, exit_layers, lengths = after((cotangent, exit_layers, lengths), normed_out)
        weight_query, weight_key, weight_value = after((weight_query, weight_key, weight_value), gathered_in.side)
        joined = jnp.concatenate([weight_query, weight_key, weight_value], 1)
    with jax.named_scope("cotangent_rows"):
        cotangent_parts = to_own(cotangent)
        about = jnp.concatenate([exit_layers[1], jnp.broadcast_to(lengths[1:], (128,))], 0)
        moved_about = lax.ppermute(about, SIDE, MOVE)
    with jax.named_scope("gather_in"):
        gathered_in.second(joined)
    with jax.named_scope("chip_weights"):
        joined, weight_out, biases, weight_up, weight_down = after(
            (joined, weight_out, biases, weight_up, weight_down), gathered_in.near
        )
        joined_core = from_core(joined)
        weight_out_core, biases_core = from_core(weight_out), from_core(biases)
        weight_up_core, weight_down_core = from_core(weight_up), from_core(weight_down)
        weight_qkv = with_layout_constraint(
            jnp.concatenate(after([joined, joined_core], gathered_in.far), 1), Layout((0, 1))
        )

    with jax.named_scope("cotangent_rows"):
        cotangent_parts, moved_about = after((cotangent_parts, moved_about), gathered_in.far)
        cotangent_own = f32(owned(cotangent, *cotangent_parts))
        positions = jnp.arange(seq_len)
        exits = jnp.where(first_core, exit_layers[0], moved_about[:seq_len])
        length = jnp.where(first_core, lengths[0], moved_about[seq_len])
        live_all = f32((positions < length) & (exits >= LAYER))
        live_own = lax.dynamic_slice_in_dim(live_all, (row * 2 + side) * own_rows, own_rows, 0)[:, None]
        sign = 1 - 2 * core
        info = jnp.stack([row, side, length, sign]).astype(jnp.int32)
        grad_own = cotangent_own * live_own
        grad_own_low = bf16(grad_own)
    with jax.named_scope("gather_in"):
        gathered_in.third()
    with jax.named_scope("project"):
        first_in = gathered_in.first_half(weight_qkv, grad_own_low)
        scale = HEAD**-0.5
        none = jnp.zeros((head_cols,), jnp.float32)
        bias_qkv = jnp.concatenate(
            [biases[:head_cols], none, biases[head_cols : 2 * head_cols]]
            + [biases_core[:head_cols], none, biases_core[head_cols : 2 * head_cols]]
        )
        scale_qkv = jnp.tile(jnp.concatenate([none + scale, none + 1.0, none + 1.0]), 2)
        bias_up_chip = jnp.concatenate([biases[2 * head_cols :], biases_core[2 * head_cols :]])

        def projected(rows):
            product = jnp.dot(rows, weight_qkv, preferred_element_type=jnp.float32)
            return bf16((product + bias_qkv) * scale_qkv)

        first_qkv = projected(first_in)
        second_in = gathered_in.second_half(first_qkv)
        qkv = jnp.concatenate([first_qkv, projected(second_in)], 0)
        hidden_in = jnp.concatenate(after([first_in, second_in], qkv), 0)
    with jax.named_scope("chip_weights"):
        weight_out_chip = jnp.concatenate([weight_out, weight_out_core], 0)
        weight_out_chip, weight_up_core, weight_down_core = after(
            (weight_out_chip, weight_up_core, weight_down_core), gathered_in.far
        )
    with jax.named_scope("gather_cotangent"):
        gathered_grad = Gather(after(grad_own_low, qkv))
    context, lse = attend_forward(info, after(qkv, weight_out_chip, weight_up_core, weight_down_core))
    with jax.named_scope("sum_attention"):
        sum_att = ProductSum(halved(context), weight_out_chip).start().second()
    with jax.named_scope("chip_weights"):
        up_own, up_core, down_own, down_core = after(
            (weight_up, weight_up_core, weight_down, weight_down_core), sum_att.far_side
        )
        weight_up_chip = jnp.concatenate([up_own, up_core], 1)
        weight_down_chip = jnp.concatenate([down_own, down_core], 0)
    with jax.named_scope("sum_attention"):
        sum_att.third(weight_up_chip, weight_down_chip)
    with jax.named_scope("gather_cotangent"):
        gathered_grad.second(sum_att.far, sum_att.near_side)
    with jax.named_scope("sum_attention"):
        attention = sum_att.total()
    with jax.named_scope("gather_mid"):
        mid_own = tokens_own + live_own * (attention + bias_out)
        normed_mid, inverse_mid, mid_out = norm_rows(mid_own, gain_mid, shift_mid)
        mid_out = bf16(mid_out)
        gathered_mid = Gather(mid_out)
    with jax.named_scope("gather_cotangent"):
        gathered_grad.third(mid_out)
    with jax.named_scope("gather_mid"):
        gathered_mid.second()
    with jax.named_scope("feed_forward"):
        live_halves = (gathered_grad.first_half(gathered_mid.near), gathered_grad.second_half(gathered_mid.near))
        grad_activated = lax.optimization_barrier(
            [
                lax.dot_general(
                    half, weight_down_chip, (((1,), (1,)), ((), ())), preferred_element_type=jnp.float32
                )
                for half in live_halves
            ]
        )
    def fed(rows, upstream):
        up_sum = jnp.dot(rows, weight_up_chip, preferred_element_type=jnp.float32) + bias_up_chip
        return bf16(jax.nn.gelu(up_sum)), bf16(jax.vjp(jax.nn.gelu, up_sum)[1](upstream)[0])

    with jax.named_scope("feed_forward"):
        first_mid = gathered_mid.third().first_half(*grad_activated)
        first_fed = fed(first_mid, grad_activated[0])
        second_mid = gathered_mid.second_half(*first_fed)
        mid_halves = (first_mid, second_mid)
        activated, grad_up_sum = zip(first_fed, fed(second_mid, grad_activated[1]))
    with jax.named_scope("sum_mid_grad"):
        sum_mid = ProductSum(grad_up_sum, weight_up_chip, ((1,), (1,))).start().second()
    with jax.named_scope("feed_forward"):
        hidden_mid, grad_live, all_activated, all_grad_up = after(
            [jnp.concatenate(pair, 0) for pair in (mid_halves, live_halves, activated, grad_up_sum)], sum_mid.far_side
        )
    with jax.named_scope("sum_branch"):
        sum_branch = ProductSum(after(activated, sum_mid.far_side), weight_down_chip)
    with jax.named_scope("grads_mlp"):
        early_up, early_act = after((all_grad_up, all_activated), sum_mid.far, sum_mid.near_side)
        grads_up = GradSum(hidden_mid, early_up[:, hidden:])
        grads_down = GradSum(grad_live, early_act[:, hidden:])
    with jax.named_scope("sum_mid_grad"):
        sum_mid.third(sum_branch.first, sum_branch.near_part, sum_branch.rest)
        mid_grad = sum_mid.total(grads_up.sent, grads_down.sent)
    with jax.named_scope("sum_branch"):
        sum_branch.start(*sum_mid.sent)
    with jax.named_scope("gather_back"):
        back_own = cotangent_own + norm_back(mid_grad, normed_mid, inverse_mid, gain_mid)
        back_live = back_own * live_own
        back_low_own = bf16(back_live)
        gathered_back = Gather(back_low_own)
    with jax.named_scope("grads_mlp"):
        grad_up = grads_up.total(all_grad_up[:, :hidden], back_low_own)
        grad_down = grads_down.total(all_activated[:, :hidden], back_low_own)
    with jax.named_scope("gather_back"):
        gathered_back.second(grad_up, grad_down)
    with jax.named_scope("dp_mlp"):
        dp_mlp = DpSum(after([grad_up, grad_down], gathered_back.near), sign)
    with jax.named_scope("sum_branch"):
        sum_branch.second(gathered_back.near)
    with jax.named_scope("early_lines"):
        early_up = after(all_grad_up, gathered_back.far)
        early_vectors = after(
            [
                column_sums(mid_grad * normed_mid),
                column_sums(mid_grad),
                column_sums(back_live),
                column_sums(grad_own),
            ],
            gathered_back.far,
        )
        column_up = column_sums(early_up)
    with jax.named_scope("gather_back"):
        gathered_back.third(*dp_mlp.sent)
    with jax.named_scope("gather_back"):
        first_back = gathered_back.first_half()

    with jax.named_scope("grad_context"):

        def to_context(rows):
            product = lax.dot_general(
                rows, weight_out_chip, (((1,), (1,)), ((), ())), preferred_element_type=jnp.float32
            )
            return bf16(product)

        context_halves = halved(context)
        first_context = to_context(first_back)
        first_product = across(first_back, context_halves[0])
        second_back = gathered_back.second_half(first_context, first_product)
        grad_context = jnp.concatenate([first_context, to_context(second_back)], 0)
    with jax.named_scope("grads_attention"):
        product_out = first_product + across(after(second_back, grad_context), context_halves[1])
        product_own, product_core = product_out[:, :head_cols], bf16(product_out[:, head_cols:])
        received_out = from_core(product_core)
    grad_qkv_core = attend_backward(info, qkv, after(grad_context, product_own, product_core), lse, 1)
    with jax.named_scope("dp_mlp"):
        dp_mlp.second(grad_qkv_core)
    with jax.named_scope("sum_branch"):
        sum_branch.third(grad_context)
    with jax.named_scope("grads_attention"):
        grads_in = GradSum(hidden_in, grad_qkv_core)
        grad_out = bf16(product_own + f32(after(received_out, grad_qkv_core)))
        columns_core = column_sums(grad_qkv_core)
        shift_core = times_columns(weight_qkv[:, width:], columns_core)
    grad_qkv_own = attend_backward(
        info,
        qkv,
        after(grad_context, grads_in.received, grad_out, shift_core, column_up, early_vectors, dp_mlp.to_ahead, sum_branch.sent),
        lse,
        0,
    )
    with jax.named_scope("sum_in_grad"):
        grad_qkv = jnp.concatenate([grad_qkv_own, grad_qkv_core], 1)
        sum_in = ProductSum(halved(grad_qkv), weight_qkv, ((1,), (1,))).start()
    with jax.named_scope("sum_in_grad"):
        sum_in.second()
    with jax.named_scope("grads_attention"):
        grad_in = grads_in.total(grad_qkv_own, sum_in.side_part)
    with jax.named_scope("dp_attention"):
        dp_attention = DpSum([grad_in, grad_out], sign)
    with jax.named_scope("dp_mlp"):
        dp_mlp.third(sum_in.side_part)
    with jax.named_scope("sum_in_grad"):
        sum_in.third(*dp_attention.sent)
    with jax.named_scope("dp_attention"):
        dp_attention.second(*sum_in.sent)

    def of_dp(values):
        return lax.dynamic_slice_in_dim(values, dp_index * part, part, 0)

    with jax.named_scope("small_sums"):
        columns_own = column_sums(after(grad_qkv_own, *sum_in.sent))
        shift_in_part = shift_core + times_columns(weight_qkv[:, :width], columns_own)
        gain_in_part = jnp.sum(f32(after(grad_in, *sum_in.sent)) * f32(weight_qkv[:, :width]), 1)
        vectors = [v.reshape(8, part) for v in (shift_in_part, *early_vectors, gain_in_part)]
        sums = [column_up[:, :hidden], columns_own[:, :head_cols], columns_own[:, 2 * head_cols :]]
        sums += [column_up[:, hidden:], columns_core[:, :head_cols], columns_core[:, 2 * head_cols :]]
        lines = jnp.concatenate(vectors + [v.reshape(8, -1) for v in sums], 1)
        lines = after(jnp.pad(lines, ((0, 0), (0, -lines.shape[1] % 128))), dp_attention.to_ahead)
        small = jnp.sum(lax.all_to_all(lines, DP, 0, 0, tiled=True), 0)
    with jax.named_scope("sum_branch"):
        branch = sum_branch.total(*sum_in.sent)
        output_own = bf16(mid_own + live_own * (branch + bias_down))
    with jax.named_scope("sum_in_grad"):
        in_grad = sum_in.total(dp_attention.to_ahead, output_own)
    with jax.named_scope("dp_attention"):
        dp_attention.third(in_grad)
    with jax.named_scope("tokens_grad"):
        tokens_grad_own = bf16(back_own + norm_back(in_grad, normed_in, inverse_in, gain_in))
        grad_tokens = f32(to_home(tokens_grad_own))
    with jax.named_scope("sum_branch"):
        output = to_home(after(output_own, tokens_grad_own))
    with jax.named_scope("small_sums"):
        to_all = small[: 6 * part]
        wide, narrow = hidden // 8, head_cols // 8
        at = 6 * part + wide + 2 * narrow
        own_biases, side_biases = small[6 * part : at], small[at : at + wide + 2 * narrow]
        dest = jnp.arange(16)[:, None]
        for_biases = jnp.where(dest == tp_index, own_biases, jnp.where(dest == (tp_index ^ 1), side_biases, 0.0))
        sent = jnp.concatenate([jnp.broadcast_to(to_all, (16, 6 * part)), for_biases], 1)
        sent = after(jnp.pad(sent, ((0, 0), (0, -sent.shape[1] % 128))), tokens_grad_own)
        small = jnp.sum(lax.all_to_all(sent, TP, 0, 0, tiled=True), 0)
        vectors = small[: 6 * part].reshape(6, part)
        up_part, query_part, value_part = (
            small[6 * part + a : 6 * part + b]
            for a, b in ((0, wide), (wide, wide + narrow), (wide + narrow, wide + 2 * narrow))
        )

    with jax.named_scope("dp_attention"):
        summed_attention = dp_attention.total(tokens_grad_own)
    with jax.named_scope("dp_mlp"):
        summed_mlp = dp_mlp.total(tokens_grad_own)

    return (
        output,
        grad_tokens,
        summed_attention[:, :head_cols],
        query_part,
        summed_attention[:, head_cols : 2 * head_cols],
        summed_attention[:, 2 * head_cols : width],
        value_part,
        summed_attention[:, width : width + head_cols].T,
        vectors[3],
        summed_mlp[:, :hidden],
        up_part,
        summed_mlp[:, hidden:].T,
        vectors[4],
        (vectors[5] - of_dp(shift_in) * vectors[0]) / of_dp(gain_in),
        vectors[0],
        vectors[1],
        vectors[2],
    )


def solution(mesh):
    names = Mesh(mesh.devices.reshape(4, 2, 2, 4, 2), EVERY)
    residual = P(DP, TP, None)
    return jax.shard_map(
        on_device,
        mesh=names,
        in_specs=(
            residual,
            P(DP),
            P(DP, None),
            P(None, TP),
            P(TP),
            P(None, TP),
            P(None, TP),
            P(TP),
            P(TP, None),
            P(),
            P(None, TP),
            P(TP),
            P(TP, None),
            P(),
            P(),
            P(),
            P(),
            P(),
            residual,
        ),
        out_specs=(
            residual,
            residual,
            P(DP, TP),
            P(EVERY),
            P(DP, TP),
            P(DP, TP),
            P(EVERY),
            P(TP, DP),
            P(DP),
            P(DP, TP),
            P(EVERY),
            P(TP, DP),
            P(DP),
            P(DP),
            P(DP),
            P(DP),
            P(DP),
        ),
        check_vma=False,
    )
```
